256 devices in a mesh: replica: 32 (over z, y_lo, core), mp: 8 (over x, y_hi).
Axes of the slice: x: 4, y: 4 (y_hi: 2, y_lo: 2; y = y_hi * 2 + y_lo), z: 8, core: 2. Of those that a mesh axis runs over, the one named last changes fastest.
Arguments:
- local_weights: bfloat16 [2, 32, 8, 128, 3072], P(None, 'replica', 'mp'), may hold values from -32 to 32, as said below
- global_params: float32 [2, 8, 128, 3072], P(None, 'mp', 'replica'), may hold values from -25 to 25
- momentum: float32 [2, 8, 128, 3072], P(None, 'mp', 'replica'), may hold values from -3 to 3
Outputs:
- mixed_weights: bfloat16 [2, 32, 8, 128, 3072], P(None, 'replica', 'mp')
- new_global: float32 [2, 8, 128, 3072], P(None, 'mp', 'replica')
- new_momentum: float32 [2, 8, 128, 3072], P(None, 'mp', 'replica')
The draws below stay inside these ranges and needn't reach their ends.
Inputs may be any that keep to these rules, and one draw needn't show every extreme that they name: `local_weights`: replica groups' weights.
All inputs are finite; a program needn't handle non-finite values.
Results may differ from the reference program's by a relative error of at most 0.0042.
Values may be sent and summed in bfloat16 or wider, within the bound.
No kernel may reach another device: no remote copies, remote signals or barrier semaphores. Data moves between devices by JAX's collectives and lax.ppermute only.
A program may use at most 64 MiB of HBM per device.

```python
import math
import jax
import jax.numpy as jnp
from jax import lax

D = 3072
ROW_DEV = 4
FRAGS = 2
REPLICAS = 32
SHARDS = 8
SHARD_ROWS = 128


def outer_field(key):
    key = jax.random.fold_in(key, 11)
    base_key = jax.random.fold_in(key, 1)
    block_key = jax.random.fold_in(key, 2)
    column_key = jax.random.fold_in(key, 3)
    rows = SHARDS * SHARD_ROWS
    place = jnp.arange(rows, dtype=jnp.float32) / max(rows - 1, 1)
    rising = (1.0 + 2.0 * place).reshape(1, SHARDS, SHARD_ROWS, 1)
    block_level = jnp.exp(jax.random.uniform(block_key, (FRAGS, SHARDS, REPLICAS), jnp.float32, -1.15, 1.15))
    block_level = jnp.repeat(block_level, ROW_DEV, axis=2)[..., None]
    column_level = jnp.exp(jax.random.uniform(column_key, (FRAGS, 1, 1, D), jnp.float32, -1.15, 1.15))
    levels = 0.3 * rising * block_level * column_level
    normal_part = jnp.clip(jax.random.normal(base_key, (FRAGS, SHARDS, SHARD_ROWS, D), jnp.float32), -2.5, 2.5)
    base = normal_part
    return base * levels


def drift_scale(key):
    key = jax.random.fold_in(key, 12)
    block_key = jax.random.fold_in(key, 1)
    row_key = jax.random.fold_in(key, 2)
    column_key = jax.random.fold_in(key, 3)
    rows = SHARDS * SHARD_ROWS
    place = jnp.arange(rows, dtype=jnp.float32) / max(rows - 1, 1)
    rising = (1.0 + 2.0 * place).reshape(1, SHARDS, SHARD_ROWS, 1)
    block_level = jnp.exp(jax.random.uniform(block_key, (FRAGS, SHARDS, REPLICAS), jnp.float32, -0.6, 0.6))
    block_level = jnp.repeat(block_level, ROW_DEV, axis=2)[..., None]
    row_level = jnp.exp(jax.random.uniform(row_key, (FRAGS, SHARDS, SHARD_ROWS, 1), jnp.float32, -0.6, 0.6))
    column_level = jnp.exp(jax.random.uniform(column_key, (FRAGS, 1, 1, D), jnp.float32, -1.15, 1.15))
    return rising * block_level * row_level * column_level / 3.8


def draw_global_params(key, part):
    outer = outer_field(key)
    return outer


def draw_local_weights(key, part):
    outer = outer_field(key)
    spread = drift_scale(key)[:, None]
    key = jax.random.fold_in(key, 31)
    shared_key = jax.random.fold_in(key, 1)
    own_key = jax.random.fold_in(key, 2)
    shared = jnp.clip(jax.random.normal(shared_key, (FRAGS, 1, SHARDS, SHARD_ROWS, D), jnp.float32), -3.0, 3.0)
    own = jnp.clip(jax.random.normal(own_key, (FRAGS, REPLICAS, SHARDS, SHARD_ROWS, D), jnp.float32), -3.0, 3.0)
    drift = spread * (0.8 * shared + 0.6 * own)
    return jnp.clip(outer[:, None] + drift, -32.0, 32.0).astype(jnp.bfloat16)


def shard_levels(key, dims, pieces, low, largest):
    def one(dim, parts):
        draws = jax.random.uniform(jax.random.fold_in(jax.random.fold_in(key, 6), dim), (parts,), jnp.float32, low / len(pieces), largest / len(pieces))
        return jnp.repeat(jnp.exp(draws), dims[dim] // parts).reshape((-1,) + (1,) * (len(dims) - dim - 1))

    loudness = one(*pieces[0])
    for cut in pieces[1:]:
        loudness = loudness * one(*cut)
    return loudness


def bell_draw(key, shape, scale, most, split=(), kind=jnp.bfloat16):
    factor_of = shard_levels(key, shape, split, -0.22, 0.18) if split else 1.0
    array = jax.random.normal(key, shape, jnp.float32) * scale * factor_of
    return jnp.minimum(jnp.maximum(array, -most), most).astype(kind)


def setup_inputs(seed: int = 0) -> dict:
    seeds = jax.random.split(jax.random.key(seed), 4)
    local_weights = draw_local_weights(jax.random.fold_in(seeds[3], 71), 0)
    global_params = draw_global_params(jax.random.fold_in(seeds[3], 71), 0)
    momentum = bell_draw(seeds[2], (FRAGS, SHARDS, SHARD_ROWS, D), 0.5, 3.0, ((1, 8), (2, 32)), jnp.float32)
    return dict(local_weights=local_weights, global_params=global_params, momentum=momentum)


def reference(local_weights, global_params, momentum):
    count = SHARDS * SHARD_ROWS * D
    max_norm = 0.5 * math.sqrt(count)
    mixed_list = []
    global_list = []
    moment_list = []
    for frag in range(FRAGS):
        total = lax.optimization_barrier(jnp.sum(local_weights[frag].astype(jnp.float32), axis=0))
        pseudo = global_params[frag] - total / REPLICAS
        square_sum = jnp.sum(pseudo * pseudo)
        factor = jnp.minimum(1.0, max_norm / (jnp.sqrt(square_sum) + 1e-06))
        clipped = factor * pseudo
        moment_next = 0.9 * momentum[frag] + clipped
        global_next = global_params[frag] - 0.7 * (clipped + 0.9 * moment_next)
        mix_source = lax.optimization_barrier(global_next.astype(jnp.bfloat16)).astype(jnp.float32)
        mixed = (0.5 * local_weights[frag].astype(jnp.float32) + 0.5 * mix_source[None]).astype(jnp.bfloat16)
        mixed_list.append(mixed)
        global_list.append(global_next)
        moment_list.append(moment_next)
    return (jnp.stack(mixed_list), jnp.stack(global_list), jnp.stack(moment_list))
```

```python
import math

import jax
import jax.numpy as jnp
from jax import lax
from jax.sharding import Mesh
from jax.sharding import PartitionSpec as P

CHIPS = ("z", "yl")
SWAP = ((0, 1), (1, 0))


def shards(local_weights, global_params, momentum):
    f32, bf16 = jnp.float32, jnp.bfloat16
    core = lax.axis_index("core")
    other = 1 - core
    chips = lax.axis_size(CHIPS)
    replicas = 2 * chips
    everywhere = chips * lax.axis_size(("x", "yh"))
    rows, width = local_weights.shape[3], local_weights.shape[4]
    share_rows = global_params.shape[2]
    block = rows // chips
    max_norm = 0.5 * math.sqrt(block * width * everywhere)

    weights = local_weights[:, 0, 0]
    state = jnp.stack((global_params[:, 0], momentum[:, 0]), axis=1)
    sent = lax.dynamic_index_in_dim(weights, other, 0, keepdims=False)
    got = lax.ppermute(sent, "core", SWAP)
    state_mine = lax.dynamic_index_in_dim(state, core, 0, keepdims=False)
    state_got = lax.ppermute(
        lax.dynamic_index_in_dim(state, other, 0, keepdims=False), "core", SWAP
    )
    own = lax.dynamic_index_in_dim(weights, core, 0, keepdims=False)
    pair = (own.astype(f32) + got.astype(f32)).astype(bf16)
    pieces = lax.all_to_all(
        pair.reshape(chips, block, width), CHIPS, 0, 0, tiled=True
    )
    total = jnp.sum(pieces.astype(f32), axis=0)
    first = core == 0
    outer, moment = jnp.where(
        first,
        jnp.concatenate((state_mine, state_got), axis=1),
        jnp.concatenate((state_got, state_mine), axis=1),
    )
    pseudo = outer - total / replicas
    part = jnp.sum(pseudo * pseudo)
    parts = lax.all_to_all(
        jnp.broadcast_to(part, (everywhere, 1, 128)),
        ("z", "yl", "x", "yh"),
        0,
        0,
        tiled=True,
    )
    square_sum = jnp.sum(parts[:, 0, 0])
    factor = jnp.minimum(1.0, max_norm / (jnp.sqrt(square_sum) + 1e-06))
    clipped = factor * pseudo
    moment_next = 0.9 * moment + clipped
    outer_next = outer - 0.7 * (clipped + 0.9 * moment_next)
    source = outer_next.astype(bf16)
    gathered = lax.all_to_all(
        jnp.broadcast_to(source, (chips, block, width)), CHIPS, 0, 0, tiled=True
    ).reshape(rows, width)
    swapped = lax.ppermute(gathered, "core", SWAP)

    state_next = jnp.stack((outer_next, moment_next))
    halves = state_next.reshape(2, 2, share_rows, width)
    keep = lax.dynamic_index_in_dim(halves, core, 1, keepdims=False)
    give = lax.dynamic_index_in_dim(halves, other, 1, keepdims=False)
    take = lax.ppermute(give, "core", SWAP)
    state_out = jnp.where(first, jnp.stack((keep, take)), jnp.stack((take, keep)))

    sources = jnp.where(
        first, jnp.stack((gathered, swapped)), jnp.stack((swapped, gathered))
    )
    mixed = (0.5 * weights.astype(f32) + 0.5 * sources.astype(f32)).astype(bf16)
    return (
        mixed[:, None, None],
        state_out[:, 0][:, None],
        state_out[:, 1][:, None],
    )


def solution(mesh):
    fine = Mesh(
        mesh.devices.reshape(8, 2, 2, 4, 2), ("z", "yl", "core", "x", "yh")
    )
    replica, mp = ("z", "yl", "core"), ("x", "yh")
    whole = P(None, replica, mp, None, None)
    outer = P(None, mp, replica, None)
    return jax.shard_map(
        shards,
        mesh=fine,
        in_specs=(whole, outer, outer),
        out_specs=(whole, outer, outer),
        check_vma=False,
    )
```

```python
import math

import jax
import jax.numpy as jnp
from jax import lax
from jax.experimental import pallas as pl
from jax.experimental.pallas import tpu as pltpu
from jax.sharding import Mesh
from jax.sharding import PartitionSpec as P

CHIPS = ("z", "yl")
SWAP = ((0, 1), (1, 0))
STEPS = (("z", 8, 4, 8), ("z", 8, 2, 4), ("z", 8, 1, 2), ("yl", 2, 1, 1))


def gather(block):
    held = block[None]
    for axis, size, step, _ in STEPS:
        pairs = [(i, i ^ step) for i in range(size)]
        held = jnp.concatenate((held, lax.ppermute(held, axis, pairs)), axis=0)
    return held


def offsets():
    places = [0]
    for _, _, _, jump in STEPS:
        places = places + [place ^ jump for place in places]
    return places


def mix_kernel(where_ref, weights_ref, mine_ref, theirs_ref, mixed_ref):
    core, me = where_ref[0], where_ref[1]
    for place, jump in enumerate(offsets()):
        chip = me ^ jump
        for frag, source_ref in ((core, mine_ref), (1 - core, theirs_ref)):
            own = weights_ref[frag, chip].astype(jnp.float32)
            source = source_ref[place].astype(jnp.float32)
            mixed_ref[frag, chip] = (0.5 * own + 0.5 * source).astype(jnp.bfloat16)


def shards(local_weights, global_params, momentum):
    f32, bf16 = jnp.float32, jnp.bfloat16
    core = lax.axis_index("core")
    other = 1 - core
    me = lax.axis_index(CHIPS)
    chips = lax.axis_size(CHIPS)
    replicas = 2 * chips
    everywhere = chips * lax.axis_size(("x", "yh"))
    rows, width = local_weights.shape[3], local_weights.shape[4]
    share_rows = global_params.shape[2]
    block = rows // chips
    max_norm = 0.5 * math.sqrt(block * width * everywhere)
    first = core == 0

    weights = local_weights[:, 0, 0]
    state = jnp.stack((global_params[:, 0], momentum[:, 0]), axis=1)
    sent = lax.dynamic_index_in_dim(weights, other, 0, keepdims=False)
    got = lax.ppermute(sent, "core", SWAP)
    state_mine = lax.dynamic_index_in_dim(state, core, 0, keepdims=False)
    state_got = lax.ppermute(
        lax.dynamic_index_in_dim(state, other, 0, keepdims=False), "core", SWAP
    )
    outer, moment = jnp.where(
        first,
        jnp.concatenate((state_mine, state_got), axis=1),
        jnp.concatenate((state_got, state_mine), axis=1),
    )
    bases = gather((outer - 0.567 * moment).astype(bf16))

    own = lax.dynamic_index_in_dim(weights, core, 0, keepdims=False)
    pair = (own.astype(f32) + got.astype(f32)).astype(bf16)
    pieces = lax.all_to_all(
        pair.reshape(chips, block, width), CHIPS, 0, 0, tiled=True
    )
    total = jnp.sum(pieces.astype(f32), axis=0)
    pseudo = outer - total / replicas
    push, bases = lax.optimization_barrier(((1.33 * pseudo).astype(bf16), bases))
    pushes = gather(push)
    part = jnp.sum(pseudo * pseudo)
    parts = lax.all_to_all(
        jnp.broadcast_to(part, (everywhere, 1, 128)),
        ("z", "yl", "x", "yh"),
        0,
        0,
        tiled=True,
    )
    square_sum = jnp.sum(parts[:, 0, 0])
    factor = jnp.minimum(1.0, max_norm / (jnp.sqrt(square_sum) + 1e-06))
    clipped = factor * pseudo
    moment_next = 0.9 * moment + clipped
    outer_next = outer - 0.7 * (clipped + 0.9 * moment_next)

    mine = (bases.astype(f32) - factor * pushes.astype(f32)).astype(bf16)
    theirs = lax.ppermute(mine, "core", SWAP)

    state_next = jnp.stack((outer_next, moment_next))
    halves = state_next.reshape(2, 2, share_rows, width)
    keep = lax.dynamic_index_in_dim(halves, core, 1, keepdims=False)
    give = lax.dynamic_index_in_dim(halves, other, 1, keepdims=False)
    take = lax.ppermute(give, "core", SWAP)
    state_out = jnp.where(first, jnp.stack((keep, take)), jnp.stack((take, keep)))

    in_vmem = pl.BlockSpec(memory_space=pltpu.VMEM)
    mixed = pl.pallas_call(
        mix_kernel,
        out_shape=jax.ShapeDtypeStruct((2, chips, block, width), bf16),
        in_specs=[pl.BlockSpec(memory_space=pltpu.SMEM), in_vmem, in_vmem, in_vmem],
        out_specs=in_vmem,
        compiler_params=pltpu.CompilerParams(vmem_limit_bytes=32 * 1024 * 1024),
        name="mix",
    )(
        jnp.stack((core, me)).astype(jnp.int32),
        weights.reshape(2, chips, block, width),
        mine,
        theirs,
    )
    return (
        mixed.reshape(local_weights.shape),
        state_out[:, 0][:, None],
        state_out[:, 1][:, None],
    )


def solution(mesh):
    fine = Mesh(
        mesh.devices.reshape(8, 2, 2, 4, 2), ("z", "yl", "core", "x", "yh")
    )
    replica, mp = ("z", "yl", "core"), ("x", "yh")
    whole = P(None, replica, mp, None, None)
    outer = P(None, mp, replica, None)
    return jax.shard_map(
        shards,
        mesh=fine,
        in_specs=(whole, outer, outer),
        out_specs=(whole, outer, outer),
        check_vma=False,
    )
```

```python
import math

import jax
import jax.numpy as jnp
from jax import lax
from jax.experimental import pallas as pl
from jax.experimental.pallas import tpu as pltpu
from jax.sharding import Mesh
from jax.sharding import PartitionSpec as P

CHIPS = ("z", "yl")
SWAP = ((0, 1), (1, 0))
STEPS = (4, 2, 1)


def gather(block):
    held = block[None]
    for step in STEPS:
        pairs = [(i, i ^ step) for i in range(8)]
        held = jnp.concatenate((held, lax.ppermute(held, "z", pairs)), axis=0)
    return held


def offsets():
    places = [0]
    for step in STEPS:
        places = places + [place ^ step for place in places]
    return places


def mix_kernel(where_ref, weights_ref, near_ref, far_ref, near2_ref, far2_ref, mixed_ref):
    core, z, yl = where_ref[0], where_ref[1], where_ref[2]
    for place, jump in enumerate(offsets()):
        row = 2 * (z ^ jump)
        for frag, side, source_ref in (
            (core, yl, near_ref),
            (core, 1 - yl, far_ref),
            (1 - core, yl, near2_ref),
            (1 - core, 1 - yl, far2_ref),
        ):
            own = weights_ref[frag, row + side].astype(jnp.float32)
            source = source_ref[place].astype(jnp.float32)
            mixed_ref[frag, row + side] = (0.5 * own + 0.5 * source).astype(
                jnp.bfloat16
            )


def shards(local_weights, global_params, momentum):
    f32, bf16 = jnp.float32, jnp.bfloat16
    core = lax.axis_index("core")
    other = 1 - core
    chips = lax.axis_size(CHIPS)
    replicas = 2 * chips
    everywhere = chips * lax.axis_size(("x", "yh"))
    rows, width = local_weights.shape[3], local_weights.shape[4]
    share_rows = global_params.shape[2]
    block = rows // chips
    max_norm = 0.5 * math.sqrt(block * width * everywhere)
    first = core == 0

    weights = local_weights[:, 0, 0]
    state = jnp.stack((global_params[:, 0], momentum[:, 0]), axis=1)
    sent = lax.dynamic_index_in_dim(weights, other, 0, keepdims=False)
    got = lax.ppermute(sent, "core", SWAP)
    state_mine = lax.dynamic_index_in_dim(state, core, 0, keepdims=False)
    state_got = lax.ppermute(
        lax.dynamic_index_in_dim(state, other, 0, keepdims=False), "core", SWAP
    )
    outer, moment = jnp.where(
        first,
        jnp.concatenate((state_mine, state_got), axis=1),
        jnp.concatenate((state_got, state_mine), axis=1),
    )
    own = lax.dynamic_index_in_dim(weights, core, 0, keepdims=False)
    pair = (own.astype(f32) + got.astype(f32)).astype(bf16)
    base = (outer - 0.567 * moment).astype(bf16)
    pair, base = lax.optimization_barrier((pair, base))
    pieces = lax.all_to_all(
        pair.reshape(chips, block, width), CHIPS, 0, 0, tiled=True
    )
    bases = gather(base)
    pieces, bases = lax.optimization_barrier((pieces, bases))
    total = jnp.sum(pieces.astype(f32), axis=0)
    pseudo = outer - total / replicas
    part = jnp.sum(pseudo * pseudo)
    parts = lax.all_to_all(
        jnp.broadcast_to(part, (everywhere, 8, 128)),
        ("z", "yl", "x", "yh"),
        0,
        0,
        tiled=True,
    )
    pushes = gather((1.33 * pseudo).astype(bf16))
    parts, pushes = lax.optimization_barrier((parts, pushes))
    square_sum = jnp.sum(parts[:, 0, 0])
    factor = jnp.minimum(1.0, max_norm / (jnp.sqrt(square_sum) + 1e-06))
    clipped = factor * pseudo
    moment_next = 0.9 * moment + clipped
    outer_next = outer - 0.7 * (clipped + 0.9 * moment_next)

    near = (bases.astype(f32) - factor * pushes.astype(f32)).astype(bf16)
    far = lax.ppermute(near, "yl", SWAP)
    near2 = lax.ppermute(near, "core", SWAP)
    far2 = lax.ppermute(far, "core", SWAP)

    state_next = jnp.stack((outer_next, moment_next))
    halves = state_next.reshape(2, 2, share_rows, width)
    keep = lax.dynamic_index_in_dim(halves, core, 1, keepdims=False)
    give = lax.dynamic_index_in_dim(halves, other, 1, keepdims=False)
    take = lax.ppermute(give, "core", SWAP)
    state_out = jnp.where(first, jnp.stack((keep, take)), jnp.stack((take, keep)))

    in_vmem = pl.BlockSpec(memory_space=pltpu.VMEM)
    mixed = pl.pallas_call(
        mix_kernel,
        out_shape=jax.ShapeDtypeStruct((2, chips, block, width), bf16),
        in_specs=[pl.BlockSpec(memory_space=pltpu.SMEM)] + [in_vmem] * 5,
        out_specs=in_vmem,
        compiler_params=pltpu.CompilerParams(vmem_limit_bytes=32 * 1024 * 1024),
        name="mix",
    )(
        jnp.stack((core, lax.axis_index("z"), lax.axis_index("yl"))),
        weights.reshape(2, chips, block, width),
        near,
        far,
        near2,
        far2,
    )
    return (
        mixed.reshape(local_weights.shape),
        state_out[:, 0][:, None],
        state_out[:, 1][:, None],
    )


def solution(mesh):
    fine = Mesh(
        mesh.devices.reshape(8, 2, 2, 4, 2), ("z", "yl", "core", "x", "yh")
    )
    replica, mp = ("z", "yl", "core"), ("x", "yh")
    whole = P(None, replica, mp, None, None)
    outer = P(None, mp, replica, None)
    return jax.shard_map(
        shards,
        mesh=fine,
        in_specs=(whole, outer, outer),
        out_specs=(whole, outer, outer),
        check_vma=False,
    )
```

```python
import functools
import math

import jax
import jax.numpy as jnp
from jax import lax
from jax.experimental import pallas as pl
from jax.experimental.pallas import tpu as pltpu
from jax.sharding import Mesh
from jax.sharding import PartitionSpec as P

CHIPS = ("z", "yl")
PLACES = ((0, 4, 2, 6), (1, 5, 3, 7))


def tied(array, *others):
    return lax.optimization_barrier((array, *others))[0]


def bring(axis, size, jump, array):
    return lax.ppermute(array, axis, [(i, i ^ jump) for i in range(size)])


def near(axis, array):
    return bring(axis, 2, 1, array)


def over_z(array, jump):
    return bring("z", 8, jump, array)


def doubled(held, jump):
    return jnp.concatenate((held, over_z(held, jump)), axis=0)


def summed(axis, size, array):
    return sum((bring(axis, size, jump, array) for jump in (1, 2, 3)), array)


def last_kernel(max_norm, where_ref, weights_ref, outer_ref, moment_ref, sums_ref, *refs):
    core, z, yl = where_ref[0], where_ref[1], where_ref[2]
    pseudo_refs, base_refs, push_refs = refs[:2], refs[2:10], refs[10:18]
    mixed_ref, new_outer_ref, new_moment_ref = refs[18:]
    norms = jnp.sqrt(sums_ref[...])
    factors = jnp.minimum(1.0, max_norm / (norms + 1e-06))
    for at in range(2):
        frag = core if at == 0 else 1 - core
        factor = factors[at : at + 1, :1]
        clipped = factor * pseudo_refs[at][...]
        moment = 0.9 * moment_ref[frag] + clipped
        new_moment_ref[frag] = moment
        new_outer_ref[frag] = outer_ref[frag] - 0.7 * (clipped + 0.9 * moment)
        for part in range(4):
            base_ref, push_ref = base_refs[4 * at + part], push_refs[4 * at + part]
            side = yl if part < 2 else 1 - yl
            for k in range(4):
                chip = 2 * (z ^ PLACES[part % 2][k]) + side
                own = weights_ref[frag, chip].astype(jnp.float32)
                base = base_ref[k].astype(jnp.float32)
                source = base - factor * push_ref[k].astype(jnp.float32)
                source = source.astype(jnp.bfloat16).astype(jnp.float32)
                mixed = 0.5 * own + 0.5 * source
                mixed_ref[frag, chip] = mixed.astype(jnp.bfloat16)


def shards(local_weights, global_params, momentum):
    f32, bf16 = jnp.float32, jnp.bfloat16
    core, yl = lax.axis_index("core"), lax.axis_index("yl")
    other = 1 - core
    first = core == 0
    chips = lax.axis_size(CHIPS)
    replicas = 2 * chips
    everywhere = chips * lax.axis_size(("x", "yh"))
    rows, width = local_weights.shape[3], local_weights.shape[4]
    share_rows = global_params.shape[2]
    block = rows // chips
    max_norm = 0.5 * math.sqrt(block * width * everywhere)

    def pick(array, index, axis=0):
        return lax.dynamic_index_in_dim(array, index, axis, keepdims=False)

    def swapped_rows(array):
        kept = pick(array, core)
        came = near("core", pick(array, other))
        return jnp.where(
            first,
            jnp.concatenate((kept, came), axis=0),
            jnp.concatenate((came, kept), axis=0),
        )

    weights = local_weights[:, 0, 0]
    outer = swapped_rows(global_params[:, 0])
    moment = swapped_rows(momentum[:, 0])
    base = (outer - 0.567 * moment).astype(bf16)[None]
    far = over_z(base, 4)
    got = near("core", pick(weights, other))
    pair = (pick(weights, core).astype(f32) + got.astype(f32)).astype(bf16)

    sides = pair.reshape(chips // 2, 2, block, width)
    give_side = pick(sides, 1 - yl, 1)
    base = jnp.concatenate((base, tied(far, give_side)), axis=0)
    got = near("yl", give_side)
    quad = (pick(sides, yl, 1).astype(f32) + got.astype(f32)).astype(bf16)
    pieces = lax.all_to_all(tied(quad, base), "z", 0, 0, tiled=True)
    base = doubled(base, 2)
    base_far = near("yl", tied(base, quad))
    bases = [base, base_far, near("core", base), near("core", base_far)]
    pieces, *bases = lax.optimization_barrier((pieces, *bases))
    base = bases[0]

    total = jnp.sum(pieces.astype(f32), axis=0)
    pseudo = outer - total / replicas
    push = (1.33 * pseudo).astype(bf16)[None]
    sums = jnp.broadcast_to(jnp.sum(pseudo * pseudo), (1, 128))

    sums = jnp.concatenate((sums, near("core", sums)), axis=0)
    sums = summed(("yl", "yh"), 4, sums)
    push = doubled(push, 4)
    more = over_z(base, 1)
    sums, push, more = lax.optimization_barrier((sums, push, more))

    sums = summed("z", 8, sums)
    push = doubled(push, 2)
    more_far = near("yl", more)
    sums, push, more, more_far = lax.optimization_barrier((sums, push, more, more_far))

    sums = sums + over_z(sums, 4)
    bases += [more, more_far, near("core", more), near("core", more_far)]
    more = over_z(push, 1)
    push_far = near("yl", push)
    halves = pseudo.reshape(2, share_rows, width)
    pseudos = [pick(halves, core), near("core", pick(halves, other))]
    sums, push, more, push_far, pseudos, bases = lax.optimization_barrier(
        (sums, push, more, push_far, pseudos, bases)
    )

    sums = summed("x", 4, sums)
    more_far = near("yl", more)
    pushes = [push, push_far, near("core", push), near("core", push_far)]
    pushes += [more, more_far, near("core", more), near("core", more_far)]
    order = (0, 4, 1, 5, 2, 6, 3, 7)
    sources = [bases[i] for i in order] + [pushes[i] for i in order]

    in_vmem = pl.BlockSpec(memory_space=pltpu.VMEM)
    state = jax.ShapeDtypeStruct((2, share_rows, width), f32)
    mixed, outer_next, moment_next = pl.pallas_call(
        functools.partial(last_kernel, max_norm),
        out_shape=(
            jax.ShapeDtypeStruct((2, chips, block, width), bf16),
            state,
            state,
        ),
        in_specs=[pl.BlockSpec(memory_space=pltpu.SMEM)] + [in_vmem] * 22,
        out_specs=(in_vmem,) * 3,
        compiler_params=pltpu.CompilerParams(vmem_limit_bytes=32 * 1024 * 1024),
        name="last",
    )(
        jnp.stack((core, lax.axis_index("z"), yl)),
        weights.reshape(2, chips, block, width),
        global_params[:, 0],
        momentum[:, 0],
        sums,
        *pseudos,
        *sources,
    )
    return (
        mixed.reshape(local_weights.shape),
        outer_next[:, None],
        moment_next[:, None],
    )


def solution(mesh):
    fine = Mesh(
        mesh.devices.reshape(8, 2, 2, 4, 2), ("z", "yl", "core", "x", "yh")
    )
    replica, mp = ("z", "yl", "core"), ("x", "yh")
    whole = P(None, replica, mp, None, None)
    outer = P(None, mp, replica, None)
    return jax.shard_map(
        shards,
        mesh=fine,
        in_specs=(whole, outer, outer),
        out_specs=(whole, outer, outer),
        check_vma=False,
    )
```

```python
import functools
import math

import jax
import jax.numpy as jnp
from jax import lax
from jax.experimental import pallas as pl
from jax.experimental.pallas import tpu as pltpu
from jax.sharding import Mesh
from jax.sharding import PartitionSpec as P

CHIPS = ("z", "yl")
EXCHANGES = (
    ("x", ((0, 1), (2, 3))),
    ("x", ((1, 2), (3, 0))),
    ("yl", ((0, 1),)),
    (("yl", "yh"), ((2, 1), (3, 0))),
    ("z", ((0, 1), (2, 3), (4, 5), (6, 7))),
    ("z", ((1, 2), (3, 4), (5, 6), (7, 0))),
    ("z", ((2, 5), (1, 6), (3, 0), (4, 7))),
)


def swap(axis, pairs, array):
    return lax.ppermute(array, axis, pairs + tuple(pair[::-1] for pair in pairs))


def over_core(array):
    return swap("core", ((0, 1),), array)


SPLIT = 2048


def total_kernel(
    replicas,
    total_ref,
    outer_ref,
    base_ref,
    pseudo_ref,
    sums_ref,
    packs_hbm,
    pack_ref,
    out_sems,
):
    width = outer_ref.shape[1]
    pseudo = outer_ref[...] - total_ref[...] / replicas
    pack_ref[:, :width] = (1.33 * pseudo).astype(jnp.bfloat16)
    pack_ref[:, width:] = base_ref[:, SPLIT:]
    copies = [
        pltpu.make_async_copy(pack_ref, packs_hbm.at[chip], out_sems.at[chip])
        for chip in range(packs_hbm.shape[0])
    ]
    for copy in copies:
        copy.start()
    pseudo_ref[...] = pseudo
    square_sum = jnp.sum(jnp.sum(pseudo * pseudo, axis=0, keepdims=True), keepdims=True)
    sums_ref[...] = jnp.broadcast_to(square_sum, sums_ref.shape)
    for copy in copies:
        copy.wait()


def last_kernel(
    max_norm,
    core_ref,
    weights_ref,
    outer_ref,
    moment_ref,
    sums_ref,
    sums2_ref,
    pseudo_ref,
    pseudo2_ref,
    packs_ref,
    packs2_ref,
    bases_hbm,
    mixed_hbm,
    new_outer_ref,
    new_moment_ref,
    bases_ref,
    mixed_ref,
    in_sems,
    out_sems,
):
    core = core_ref[0]
    chips, _, width = weights_ref.shape[1:]
    parts = out_sems.shape[0]
    step = chips // parts
    loads = []
    for part in range(parts):
        some = pl.ds(part * step, step)
        loads.append(
            pltpu.make_async_copy(
                bases_hbm.at[some], bases_ref.at[some], in_sems.at[part]
            )
        )
        loads[-1].start()
    sides = []
    for frag, square_sum_ref, rows_ref, pack_ref in (
        (core, sums_ref, pseudo_ref, packs_ref),
        (1 - core, sums2_ref, pseudo2_ref, packs2_ref),
    ):
        norms = jnp.sqrt(square_sum_ref[...])
        factor = jnp.minimum(1.0, max_norm / (norms + 1e-06))[:, :1]
        sides.append((frag, factor, pack_ref))
        clipped = factor * rows_ref[...]
        moment = 0.9 * moment_ref[frag] + clipped
        new_moment_ref[frag] = moment
        new_outer_ref[frag] = outer_ref[frag] - 0.7 * (clipped + 0.9 * moment)
    stores = []
    for part in range(parts):
        loads[part].wait()
        for at, (frag, factor, pack_ref) in enumerate(sides):
            for chip in range(part * step, part * step + step):
                for low, high, base in (
                    (0, SPLIT, bases_ref[chip, frag]),
                    (SPLIT, width, pack_ref[chip, :, width:]),
                ):
                    own = weights_ref[frag, chip, :, low:high].astype(jnp.float32)
                    push = pack_ref[chip, :, low:high].astype(jnp.float32)
                    source = base.astype(jnp.float32) - factor * push
                    source = source.astype(jnp.bfloat16).astype(jnp.float32)
                    mixed = 0.5 * (own + source)
                    mixed_ref[at, chip, :, low:high] = mixed.astype(jnp.bfloat16)
            some = pl.ds(part * step, step)
            stores.append(
                pltpu.make_async_copy(
                    mixed_ref.at[at, some],
                    mixed_hbm.at[frag, some],
                    out_sems.at[part, at],
                )
            )
            stores[-1].start()
    for store in stores:
        store.wait()


def shards(local_weights, global_params, momentum):
    f32, bf16 = jnp.float32, jnp.bfloat16
    core = lax.axis_index("core")
    other = 1 - core
    first = core == 0
    chips = lax.axis_size(CHIPS)
    replicas = 2 * chips
    everywhere = chips * lax.axis_size(("x", "yh"))
    rows, width = local_weights.shape[3], local_weights.shape[4]
    share_rows = global_params.shape[2]
    block = rows // chips
    max_norm = 0.5 * math.sqrt(block * width * everywhere)

    def pick(array, index, axis=0):
        return lax.dynamic_index_in_dim(array, index, axis, keepdims=False)

    def swapped_rows(array):
        kept = pick(array, core)
        came = over_core(pick(array, other))
        return jnp.where(
            first,
            jnp.concatenate((kept, came), axis=0),
            jnp.concatenate((came, kept), axis=0),
        )

    weights = local_weights[:, 0, 0]
    outer = swapped_rows(global_params[:, 0])
    moment = swapped_rows(momentum[:, 0])
    base = (outer - 0.567 * moment).astype(bf16)
    got = over_core(pick(weights, other))
    in_vmem = pl.BlockSpec(memory_space=pltpu.VMEM)
    in_hbm = pl.BlockSpec(memory_space=pl.ANY)
    in_smem = pl.BlockSpec(memory_space=pltpu.SMEM)
    pair = (pick(weights, core).astype(f32) + got.astype(f32)).astype(bf16)
    pair, base = lax.optimization_barrier((pair, base))
    bases = lax.all_gather(
        base[:, :SPLIT], ("z", "yl", "core"), axis=0, tiled=False
    )
    pieces = lax.all_to_all(
        pair.reshape(chips, block, width), CHIPS, 0, 0, tiled=True
    )
    extended = 2 * width - SPLIT
    pseudo, sums, pack = pl.pallas_call(
        functools.partial(total_kernel, replicas),
        out_shape=(
            pltpu.VMEM((block, width), f32),
            pltpu.VMEM((1, 128), f32),
            jax.ShapeDtypeStruct((chips, block, extended), bf16),
        ),
        in_specs=[in_vmem] * 3,
        out_specs=(in_vmem, in_vmem, in_hbm),
        scratch_shapes=[
            pltpu.VMEM((block, extended), bf16),
            pltpu.SemaphoreType.DMA((chips,)),
        ],
        name="total",
    )(jnp.sum(pieces.astype(f32), axis=0), outer, base)
    packs = lax.all_to_all(pack, CHIPS, 0, 0, tiled=True)
    halves = pseudo.reshape(2, share_rows, width)
    pseudo2 = over_core(pick(halves, other))
    for step, (axis, pairs) in enumerate(EXCHANGES):
        if step == 5:
            sums, bases = lax.optimization_barrier((sums, bases))
        if step == 6:
            sums, packs = lax.optimization_barrier((sums, packs))
        sums = sums + swap(axis, pairs, sums)
    packs2 = over_core(packs)
    sums2 = over_core(sums)

    state = jax.ShapeDtypeStruct((2, share_rows, width), f32)
    mixed, outer_next, moment_next = pl.pallas_call(
        functools.partial(last_kernel, max_norm),
        out_shape=(
            jax.ShapeDtypeStruct((2, chips, block, width), bf16),
            state,
            state,
        ),
        in_specs=[in_smem] + [in_vmem] * 9 + [in_hbm],
        out_specs=(in_hbm, in_vmem, in_vmem),
        scratch_shapes=[
            pltpu.VMEM((chips, 2, block, SPLIT), bf16),
            pltpu.VMEM((2, chips, block, width), bf16),
            pltpu.SemaphoreType.DMA((4,)),
            pltpu.SemaphoreType.DMA((4, 2)),
        ],
        compiler_params=pltpu.CompilerParams(vmem_limit_bytes=16 * 1024 * 1024),
        name="last",
    )(
        core[None],
        weights.reshape(2, chips, block, width),
        global_params[:, 0],
        momentum[:, 0],
        sums,
        sums2,
        pick(halves, core),
        pseudo2,
        packs,
        packs2,
        pltpu.with_memory_space_constraint(
            bases.reshape(chips, 2, block, SPLIT), pltpu.HBM
        ),
    )
    return (
        mixed.reshape(local_weights.shape),
        outer_next[:, None],
        moment_next[:, None],
    )


def solution(mesh):
    fine = Mesh(
        mesh.devices.reshape(8, 2, 2, 4, 2), ("z", "yl", "core", "x", "yh")
    )
    replica, mp = ("z", "yl", "core"), ("x", "yh")
    whole = P(None, replica, mp, None, None)
    outer = P(None, mp, replica, None)
    return jax.shard_map(
        shards,
        mesh=fine,
        in_specs=(whole, outer, outer),
        out_specs=(whole, outer, outer),
        check_vma=False,
    )
```

```python
import functools
import math

import jax
import jax.numpy as jnp
from jax import lax
from jax.experimental import pallas as pl
from jax.experimental.pallas import tpu as pltpu
from jax.sharding import Mesh
from jax.sharding import PartitionSpec as P

CHIPS = ("z", "yl")
EVERYWHERE = ("z", "yl", "x", "yh")
NEAR, NEXT = (0, 4, 2, 6), (1, 5, 3, 7)
LINES = 1
ANY = pl.BlockSpec(memory_space=pl.ANY)
SMEM = pl.BlockSpec(memory_space=pltpu.SMEM)
SMALL = pltpu.CompilerParams(vmem_limit_bytes=12 * 1024 * 1024)
VMEM = pl.BlockSpec(memory_space=pltpu.VMEM)


def over(axis, size, jump, array):
    return lax.ppermute(array, axis, [(i, i ^ jump) for i in range(size)])


def over_core(array):
    return over("core", 2, 1, array)


def over_y(array):
    return over("yl", 2, 1, array)


def over_z(array, jump):
    return over("z", 8, jump, array)


def total_kernel(
    replicas, total_ref, outer_ref, moment_ref, pseudo_ref, pack_ref, sums_hbm, sums_ref, sem
):
    outer = outer_ref[...]
    pseudo = outer - total_ref[...] / replicas
    square_sum = jnp.sum(jnp.sum(pseudo * pseudo, axis=0, keepdims=True), keepdims=True)
    sums_ref[...] = jnp.broadcast_to(square_sum[None], sums_ref.shape)
    copy = pltpu.make_async_copy(sums_ref, sums_hbm, sem)
    copy.start()
    pseudo_ref[...] = pseudo
    pack_ref[0] = (outer - 0.567 * moment_ref[...]).astype(jnp.bfloat16)
    pack_ref[1] = (1.33 * pseudo).astype(jnp.bfloat16)
    copy.wait()


def source_kernel(max_norm, sums_ref, *refs):
    source_ref, factor_ref = refs[-2:]
    square_sum = jnp.sum(sums_ref[:, 0, :], axis=0, keepdims=True)
    factor = jnp.minimum(1.0, max_norm / (jnp.sqrt(square_sum) + 1e-06))
    factor_ref[...] = factor
    for place, pack_ref in enumerate(refs[:-2]):
        base = pack_ref[0].astype(jnp.float32)
        push = pack_ref[1].astype(jnp.float32)
        source_ref[place] = (base - factor[:, :1] * push).astype(jnp.bfloat16)


def state_kernel(
    core,
    outer_ref,
    moment_ref,
    factor_ref,
    factor2_ref,
    pseudo_ref,
    pseudo2_ref,
    new_outer_ref,
    new_moment_ref,
):
    for frag, scale_ref, rows_ref in (
        (core, factor_ref, pseudo_ref),
        (1 - core, factor2_ref, pseudo2_ref),
    ):
        clipped = scale_ref[:, :1] * rows_ref[...]
        moment = 0.9 * moment_ref[frag] + clipped
        new_moment_ref[frag] = moment
        new_outer_ref[frag] = outer_ref[frag] - 0.7 * (clipped + 0.9 * moment)


def mix_kernel(jobs, where_ref, weights_ref, *refs):
    core, z, yl = where_ref[0], where_ref[1], where_ref[2]
    mixed_hbm, mixed_ref, sems = refs[-3:]
    stores = []
    for number, (other_frag, other_side, places) in enumerate(jobs):
        frag = 1 - core if other_frag else core
        side = 1 - yl if other_side else yl
        for k, jump in enumerate(places):
            chip = 2 * (z ^ jump) + side
            own = weights_ref[frag, chip].astype(jnp.float32)
            source = refs[number][k].astype(jnp.float32)
            mixed_ref[number, k] = (0.5 * own + 0.5 * source).astype(jnp.bfloat16)
            stores.append(
                pltpu.make_async_copy(
                    mixed_ref.at[number, k], mixed_hbm.at[frag, chip], sems.at[number, k]
                )
            )
            stores[-1].start()
    for store in stores:
        store.wait()


def shards(local_weights, global_params, momentum):
    f32, bf16 = jnp.float32, jnp.bfloat16
    core, z, yl = (lax.axis_index(axis) for axis in ("core", "z", "yl"))
    other = 1 - core
    first = core == 0
    chips = lax.axis_size(CHIPS)
    replicas = 2 * chips
    everywhere = lax.axis_size(EVERYWHERE)
    rows, width = local_weights.shape[3], local_weights.shape[4]
    share_rows = global_params.shape[2]
    block = rows // chips
    max_norm = 0.5 * math.sqrt(block * width * everywhere)

    def pick(array, index, axis=0):
        return lax.dynamic_index_in_dim(array, index, axis, keepdims=False)

    def swapped_rows(array):
        kept = pick(array, core)
        came = over_core(pick(array, other))
        return jnp.where(
            first,
            jnp.concatenate((kept, came), axis=0),
            jnp.concatenate((came, kept), axis=0),
        )

    weights = local_weights[:, 0, 0]
    outer = swapped_rows(global_params[:, 0])
    moment = swapped_rows(momentum[:, 0])
    got = over_core(pick(weights, other))
    pair = (pick(weights, core).astype(f32) + got.astype(f32)).astype(bf16)
    pieces = lax.all_to_all(
        pair.reshape(chips, block, width), CHIPS, 0, 0, tiled=True
    )
    pseudo, pack, sums = pl.pallas_call(
        functools.partial(total_kernel, replicas),
        out_shape=(
            pltpu.VMEM((block, width), f32),
            pltpu.VMEM((2, block, width), bf16),
            jax.ShapeDtypeStruct((everywhere, LINES, 128), f32),
        ),
        in_specs=[VMEM] * 3,
        out_specs=(VMEM, VMEM, ANY),
        scratch_shapes=[
            pltpu.VMEM((everywhere, LINES, 128), f32),
            pltpu.SemaphoreType.DMA,
        ],
        compiler_params=SMALL,
        name="total",
    )(jnp.sum(pieces.astype(f32), axis=0), outer, moment)

    sums = lax.all_to_all(sums, EVERYWHERE, 0, 0, tiled=True)
    packs = [over_z(pack, jump) for jump in NEAR[1:]]
    halves = pseudo.reshape(2, share_rows, width)
    pseudo2 = over_core(pick(halves, other))
    packs, pseudo2 = lax.optimization_barrier((packs, pseudo2))
    near, factor = pl.pallas_call(
        functools.partial(source_kernel, max_norm),
        out_shape=(
            pltpu.VMEM((len(NEAR), block, width), bf16),
            pltpu.VMEM((1, 128), f32),
        ),
        in_specs=[VMEM] * (1 + len(NEAR)),
        out_specs=(VMEM, VMEM),
        compiler_params=SMALL,
        name="source",
    )(sums, pack, *packs)

    far = over_y(near)
    after = over_z(near, 1)
    after_far = over_y(after)
    factor2 = over_core(factor)

    where = jnp.stack((core, z, yl))
    blocks = weights.reshape(2, chips, block, width)

    jobs = (
        (False, False, NEAR),
        (True, False, NEAR),
        (False, True, NEAR),
        (True, True, NEAR),
        (False, False, NEXT),
        (True, False, NEXT),
    )
    last_jobs = ((False, True, NEXT), (True, True, NEXT))

    def scratch(number):
        return [
            pltpu.VMEM((number, len(NEAR), block, width), bf16),
            pltpu.SemaphoreType.DMA((number, len(NEAR))),
        ]

    def mix_and_state(where_ref, weights_ref, *refs):
        count = len(jobs)
        states, (mixed_hbm, *news), room = refs[count:-5], refs[-5:-2], refs[-2:]
        mix_kernel(jobs, where_ref, weights_ref, *refs[:count], mixed_hbm, *room)
        state_kernel(where_ref[0], *states, *news)

    def mix_last(where_ref, weights_ref, *refs):
        mix_kernel(last_jobs, where_ref, weights_ref, *refs[:2], *refs[-3:])

    state = jax.ShapeDtypeStruct((2, share_rows, width), f32)
    mixed_type = jax.ShapeDtypeStruct(blocks.shape, bf16)
    mixed, outer_next, moment_next = pl.pallas_call(
        mix_and_state,
        out_shape=(mixed_type, state, state),
        in_specs=[SMEM] + [VMEM] * (1 + len(jobs) + 6),
        out_specs=(ANY, VMEM, VMEM),
        scratch_shapes=scratch(len(jobs)),
        compiler_params=SMALL,
        name="mix",
    )(
        where,
        blocks,
        near,
        over_core(near),
        far,
        over_core(far),
        after,
        over_core(after),
        global_params[:, 0],
        momentum[:, 0],
        factor,
        factor2,
        pick(halves, core),
        pseudo2,
    )
    after_far, mixed = lax.optimization_barrier((after_far, mixed))
    mixed = pl.pallas_call(
        mix_last,
        out_shape=mixed_type,
        in_specs=[SMEM, VMEM, VMEM, VMEM, ANY],
        out_specs=ANY,
        scratch_shapes=scratch(len(last_jobs)),
        input_output_aliases={4: 0},
        compiler_params=SMALL,
        name="mix_last",
    )(where, blocks, after_far, over_core(after_far), mixed)
    return (
        mixed.reshape(local_weights.shape),
        outer_next[:, None],
        moment_next[:, None],
    )


def solution(mesh):
    fine = Mesh(
        mesh.devices.reshape(8, 2, 2, 4, 2), ("z", "yl", "core", "x", "yh")
    )
    replica, mp = ("z", "yl", "core"), ("x", "yh")
    whole = P(None, replica, mp, None, None)
    outer = P(None, mp, replica, None)
    return jax.shard_map(
        shards,
        mesh=fine,
        in_specs=(whole, outer, outer),
        out_specs=(whole, outer, outer),
        check_vma=False,
    )
```

```python
import functools
import math

import jax
import jax.numpy as jnp
from jax import lax
from jax.experimental import pallas as pl
from jax.experimental.pallas import tpu as pltpu
from jax.sharding import Mesh
from jax.sharding import PartitionSpec as P

CHIPS = ("zh", "zl", "yl")
EVERYWHERE = ("zh", "zl", "yl", "x", "yh")
GROUPS = ("zl", "yl", "x", "yh")
JUMPS = (0, 2, 1, 3)
EXTRA = 128
PARTS = 4
ANY = pl.BlockSpec(memory_space=pl.ANY)
SMEM = pl.BlockSpec(memory_space=pltpu.SMEM)
SMALL = pltpu.CompilerParams(vmem_limit_bytes=12 * 1024 * 1024)
VMEM = pl.BlockSpec(memory_space=pltpu.VMEM)


def over(axis, size, jump, array):
    return lax.ppermute(array, axis, [(i, i ^ jump) for i in range(size)])


def over_core(array):
    return over("core", 2, 1, array)


def over_y(array):
    return over("yl", 2, 1, array)


def over_z(array):
    return over("zl", 2, 1, array)


def cut_kernel(which_ref, weights_hbm, cut_ref, sems):
    step = cut_ref.shape[0] // PARTS
    copies = []
    for part in range(PARTS):
        some = pl.ds(part * step, step)
        copies.append(
            pltpu.make_async_copy(
                weights_hbm.at[which_ref[0], some], cut_ref.at[some], sems.at[part]
            )
        )
        copies[-1].start()
    for copy in copies:
        copy.wait()


def pair_kernel(core_ref, weights_ref, got_ref, pair_hbm, pair_ref, sems):
    step = got_ref.shape[0] // PARTS
    copies = []
    for part in range(PARTS):
        some = pl.ds(part * step, step)
        own = weights_ref[core_ref[0], some].astype(jnp.float32)
        pair = own + got_ref[some].astype(jnp.float32)
        pair_ref[some] = pair.astype(jnp.bfloat16)
        copies.append(
            pltpu.make_async_copy(
                pair_ref.at[some], pair_hbm.at[some], sems.at[part]
            )
        )
        copies[-1].start()
    for copy in copies:
        copy.wait()


def total_kernel(replicas, total_ref, outer_ref, moment_ref, pseudo_ref, pack_ref):
    outer = outer_ref[...]
    width = outer.shape[1]
    pseudo = outer - total_ref[...] / replicas
    pseudo_ref[...] = pseudo
    pack_ref[0, :, :width] = (outer - 0.567 * moment_ref[...]).astype(jnp.bfloat16)
    pack_ref[1, :, :width] = (1.33 * pseudo).astype(jnp.bfloat16)
    square_sum = jnp.sum(jnp.sum(pseudo * pseudo, axis=0, keepdims=True), keepdims=True)
    high = square_sum.astype(jnp.bfloat16).astype(jnp.float32)
    middle = (square_sum - high).astype(jnp.bfloat16).astype(jnp.float32)
    low = square_sum - high - middle
    shape = (outer.shape[0], EXTRA)
    row = lax.broadcasted_iota(jnp.int32, shape, 0)
    lines = jnp.where(row == 0, high, jnp.where(row == 1, middle, low))
    lines = jnp.where(row < 3, lines, 0.0).astype(jnp.bfloat16)
    pack_ref[0, :, width:] = lines
    pack_ref[1, :, width:] = lines


def join_kernel(*refs):
    pack_refs = refs[: len(JUMPS)]
    joined_ref, sums_hbm, sums_ref, sem = refs[len(JUMPS) :]
    width = joined_ref.shape[3]
    lines = sum(ref[0, :, width:].astype(jnp.float32) for ref in pack_refs)
    sums_ref[...] = jnp.broadcast_to(
        jnp.sum(lines, axis=0, keepdims=True)[None], sums_ref.shape
    )
    copy = pltpu.make_async_copy(sums_ref, sums_hbm, sem)
    copy.start()
    for place, ref in enumerate(pack_refs):
        joined_ref[place] = ref[:, :, :width]
    copy.wait()


def source_kernel(max_norm, sums_ref, *refs):
    joined_refs, (source_ref, factor_ref) = refs[:-2], refs[-2:]
    square_sum = jnp.sum(sums_ref[:, 0, :], axis=0, keepdims=True)
    factor = jnp.minimum(1.0, max_norm / (jnp.sqrt(square_sum) + 1e-06))
    factor_ref[...] = factor
    for number, joined_ref in enumerate(joined_refs):
        for place in range(len(JUMPS)):
            base = joined_ref[place, 0].astype(jnp.float32)
            push = joined_ref[place, 1].astype(jnp.float32)
            source = base - factor[:, :1] * push
            source_ref[number, place] = source.astype(jnp.bfloat16)


def state_kernel(
    core,
    outer_ref,
    moment_ref,
    factor_ref,
    factor2_ref,
    pseudo_ref,
    pseudo2_ref,
    new_outer_ref,
    new_moment_ref,
):
    for frag, scale_ref, rows_ref in (
        (core, factor_ref, pseudo_ref),
        (1 - core, factor2_ref, pseudo2_ref),
    ):
        clipped = scale_ref[:, :1] * rows_ref[...]
        moment = 0.9 * moment_ref[frag] + clipped
        new_moment_ref[frag] = moment
        new_outer_ref[frag] = outer_ref[frag] - 0.7 * (clipped + 0.9 * moment)


def mix_kernel(jobs, where_ref, weights_ref, *refs):
    core, zh, zl, yl = (where_ref[i] for i in range(4))
    mixed_hbm, mixed_ref, sems = refs
    stores = []
    for number, (source_ref, other_frag, other_z, other_y) in enumerate(jobs):
        frag = 1 - core if other_frag else core
        low = (1 - zl if other_z else zl) * 2 + (1 - yl if other_y else yl)
        for k, jump in enumerate(JUMPS):
            chip = 4 * (zh ^ jump) + low
            own = weights_ref[frag, chip].astype(jnp.float32)
            source = source_ref[k].astype(jnp.float32)
            mixed_ref[number, k] = (0.5 * own + 0.5 * source).astype(jnp.bfloat16)
            stores.append(
                pltpu.make_async_copy(
                    mixed_ref.at[number, k], mixed_hbm.at[frag, chip], sems.at[number, k]
                )
            )
            stores[-1].start()
    for store in stores:
        store.wait()


def shards(local_weights, global_params, momentum):
    f32, bf16 = jnp.float32, jnp.bfloat16
    core = lax.axis_index("core")
    other = 1 - core
    first = core == 0
    chips = lax.axis_size(CHIPS)
    replicas = 2 * chips
    everywhere = lax.axis_size(EVERYWHERE)
    rows, width = local_weights.shape[3], local_weights.shape[4]
    share_rows = global_params.shape[2]
    block = rows // chips
    max_norm = 0.5 * math.sqrt(block * width * everywhere)

    def pick(array, index, axis=0):
        return lax.dynamic_index_in_dim(array, index, axis, keepdims=False)

    def swapped_rows(array):
        kept = pick(array, core)
        came = over_core(pick(array, other))
        return jnp.where(
            first,
            jnp.concatenate((kept, came), axis=0),
            jnp.concatenate((came, kept), axis=0),
        )

    weights = local_weights[:, 0, 0]
    outer = swapped_rows(global_params[:, 0])
    moment = swapped_rows(momentum[:, 0])
    sent = pl.pallas_call(
        cut_kernel,
        out_shape=pltpu.VMEM((rows, width), bf16),
        in_specs=[SMEM, ANY],
        out_specs=VMEM,
        scratch_shapes=[pltpu.SemaphoreType.DMA((PARTS,))],
        compiler_params=SMALL,
        name="cut",
    )(other[None], pltpu.with_memory_space_constraint(weights, pltpu.HBM))
    pair = pl.pallas_call(
        pair_kernel,
        out_shape=jax.ShapeDtypeStruct((rows, width), bf16),
        in_specs=[SMEM, VMEM, VMEM],
        out_specs=ANY,
        scratch_shapes=[
            pltpu.VMEM((rows, width), bf16),
            pltpu.SemaphoreType.DMA((PARTS,)),
        ],
        compiler_params=SMALL,
        name="pair",
    )(core[None], weights, over_core(sent))
    pieces = lax.all_to_all(
        pair.reshape(chips, block, width), CHIPS, 0, 0, tiled=True
    )
    pseudo, pack = pl.pallas_call(
        functools.partial(total_kernel, replicas),
        out_shape=(
            pltpu.VMEM((block, width), f32),
            pltpu.VMEM((2, block, width + EXTRA), bf16),
        ),
        in_specs=[VMEM] * 3,
        out_specs=(VMEM, VMEM),
        compiler_params=SMALL,
        name="total",
    )(jnp.sum(pieces.astype(f32), axis=0), outer, moment)
    halves = pseudo.reshape(2, share_rows, width)
    pseudo2 = over_core(pick(halves, other))

    packs = [pack] + [over("zh", 4, jump, pack) for jump in JUMPS[1:]]
    packs, pseudo2 = lax.optimization_barrier((packs, pseudo2))
    groups = lax.axis_size(GROUPS)
    joined, sums = pl.pallas_call(
        join_kernel,
        out_shape=(
            pltpu.VMEM((len(JUMPS), 2, block, width), bf16),
            jax.ShapeDtypeStruct((groups, 1, EXTRA), f32),
        ),
        in_specs=[VMEM] * len(JUMPS),
        out_specs=(VMEM, ANY),
        scratch_shapes=[
            pltpu.VMEM((groups, 1, EXTRA), f32),
            pltpu.SemaphoreType.DMA,
        ],
        compiler_params=SMALL,
        name="join",
    )(*packs)

    sums = lax.all_to_all(sums, GROUPS, 0, 0, tiled=True)
    after = over_z(joined)
    far = over_y(joined)
    sources, factor = pl.pallas_call(
        functools.partial(source_kernel, max_norm),
        out_shape=(
            pltpu.VMEM((3, len(JUMPS), block, width), bf16),
            pltpu.VMEM((1, EXTRA), f32),
        ),
        in_specs=[VMEM] * 4,
        out_specs=(VMEM, VMEM),
        compiler_params=SMALL,
        name="source",
    )(sums, joined, after, far)

    left = over_y(sources[1, :, :, : width // 2])
    right = over_z(sources[2, :, :, width // 2 :])
    sources2 = over_core(sources)
    factor2 = over_core(factor)

    where = jnp.stack([core] + [lax.axis_index(axis) for axis in CHIPS])
    blocks = weights.reshape(2, chips, block, width)

    def scratch(number):
        return [
            pltpu.VMEM((number, len(JUMPS), block, width), bf16),
            pltpu.SemaphoreType.DMA((number, len(JUMPS))),
        ]

    def mix_and_state(where_ref, weights_ref, sources_ref, sources2_ref, *refs):
        states, (mixed_hbm, *news), room = refs[:6], refs[6:9], refs[9:]
        jobs = [
            (ref.at[number], ref is sources2_ref, number == 1, number == 2)
            for number in range(3)
            for ref in (sources_ref, sources2_ref)
        ]
        mix_kernel(jobs, where_ref, weights_ref, mixed_hbm, *room)
        state_kernel(where_ref[0], *states, *news)

    def mix_last(where_ref, weights_ref, source_ref, source2_ref, _, *refs):
        jobs = [(source_ref, False, True, True), (source2_ref, True, True, True)]
        mix_kernel(jobs, where_ref, weights_ref, *refs)

    state = jax.ShapeDtypeStruct((2, share_rows, width), f32)
    mixed_type = jax.ShapeDtypeStruct(blocks.shape, bf16)
    mixed, outer_next, moment_next = pl.pallas_call(
        mix_and_state,
        out_shape=(mixed_type, state, state),
        in_specs=[SMEM] + [VMEM] * 9,
        out_specs=(ANY, VMEM, VMEM),
        scratch_shapes=scratch(6),
        compiler_params=SMALL,
        name="mix",
    )(
        where,
        blocks,
        sources,
        sources2,
        global_params[:, 0],
        momentum[:, 0],
        factor,
        factor2,
        pick(halves, core),
        pseudo2,
    )
    left, right, mixed = lax.optimization_barrier((left, right, mixed))
    diagonal = jnp.concatenate((left, right), axis=2)
    mixed = pl.pallas_call(
        mix_last,
        out_shape=mixed_type,
        in_specs=[SMEM, VMEM, VMEM, VMEM, ANY],
        out_specs=ANY,
        scratch_shapes=scratch(2),
        input_output_aliases={4: 0},
        compiler_params=SMALL,
        name="mix_last",
    )(where, blocks, diagonal, over_core(diagonal), mixed)
    return (
        mixed.reshape(local_weights.shape),
        outer_next[:, None],
        moment_next[:, None],
    )


def solution(mesh):
    fine = Mesh(
        mesh.devices.reshape(4, 2, 2, 2, 4, 2), ("zh", "zl", "yl", "core", "x", "yh")
    )
    replica, mp = ("zh", "zl", "yl", "core"), ("x", "yh")
    whole = P(None, replica, mp, None, None)
    outer = P(None, mp, replica, None)
    return jax.shard_map(
        shards,
        mesh=fine,
        in_specs=(whole, outer, outer),
        out_specs=(whole, outer, outer),
        check_vma=False,
    )
```

```python
import functools
import math

import jax
import jax.numpy as jnp
from jax import lax
from jax.experimental import pallas as pl
from jax.experimental.pallas import tpu as pltpu
from jax.sharding import Mesh
from jax.sharding import PartitionSpec as P

CHIPS = ("zh", "zl", "yl")
EVERYWHERE = ("zh", "zl", "yl", "x", "yh")
GROUPS = ("zl", "yl", "x", "yh")
JUMPS = (0, 2, 1, 3)
EXTRA = 128
PARTS = 4
ANY = pl.BlockSpec(memory_space=pl.ANY)
SMEM = pl.BlockSpec(memory_space=pltpu.SMEM)
SMALL = pltpu.CompilerParams(vmem_limit_bytes=12 * 1024 * 1024)
VMEM = pl.BlockSpec(memory_space=pltpu.VMEM)


def over(axis, size, jump, array):
    return lax.ppermute(array, axis, [(i, i ^ jump) for i in range(size)])


def over_core(array):
    return over("core", 2, 1, array)


def over_y(array):
    return over("yl", 2, 1, array)


def over_z(array):
    return over("zl", 2, 1, array)


def cut_kernel(which_ref, weights_hbm, cut_ref, sems):
    step = cut_ref.shape[0] // PARTS
    copies = []
    for part in range(PARTS):
        some = pl.ds(part * step, step)
        copies.append(
            pltpu.make_async_copy(
                weights_hbm.at[which_ref[0], some], cut_ref.at[some], sems.at[part]
            )
        )
        copies[-1].start()
    for copy in copies:
        copy.wait()


def pair_of(weights_ref, got_ref, core, at, columns):
    own = weights_ref[(core, *at)][:, columns].astype(jnp.float32)
    return own + got_ref[at][:, columns].astype(jnp.float32)


def first_kernel(where_ref, weights_ref, got_ref, left_ref, right_ref):
    core, zl, yl = where_ref[0], where_ref[2], where_ref[3]
    half = left_ref.shape[3]
    for zh in range(4):
        for bit in range(2):
            pair = pair_of(weights_ref, got_ref, core, (zh, bit, 1 - yl), slice(0, half))
            left_ref[zh, bit] = pair.astype(jnp.bfloat16)
            pair = pair_of(
                weights_ref, got_ref, core, (zh, 1 - zl, bit), slice(half, None)
            )
            right_ref[zh, bit] = pair.astype(jnp.bfloat16)


def second_kernel(where_ref, weights_ref, got_ref, left_ref, right_ref, left2_ref, right2_ref):
    core, zl, yl = where_ref[0], where_ref[2], where_ref[3]
    half = left_ref.shape[3]
    for zh in range(4):
        pair = pair_of(weights_ref, got_ref, core, (zh, 1 - zl, yl), slice(0, half))
        quad = pair + left_ref[zh, 1 - zl].astype(jnp.float32)
        left2_ref[zh] = quad.astype(jnp.bfloat16)
        pair = pair_of(weights_ref, got_ref, core, (zh, zl, 1 - yl), slice(half, None))
        quad = pair + right_ref[zh, 1 - yl].astype(jnp.float32)
        right2_ref[zh] = quad.astype(jnp.bfloat16)


def third_kernel(
    where_ref, weights_ref, got_ref, left_ref, right_ref, left2_ref, right2_ref, *outs
):
    core, zh, zl, yl = (where_ref[i] for i in range(4))
    half = left_ref.shape[3]
    for jump, out_ref in zip(JUMPS, outs):
        to = zh ^ jump
        at = (to, zl, yl)
        left = pair_of(weights_ref, got_ref, core, at, slice(0, half))
        left += left_ref[to, zl].astype(jnp.float32)
        left += left2_ref[to].astype(jnp.float32)
        right = pair_of(weights_ref, got_ref, core, at, slice(half, None))
        right += right_ref[to, yl].astype(jnp.float32)
        right += right2_ref[to].astype(jnp.float32)
        out_ref[:, :half] = left.astype(out_ref.dtype)
        out_ref[:, half:] = right.astype(out_ref.dtype)


def split_lines(value, rows):
    high = value.astype(jnp.bfloat16).astype(jnp.float32)
    middle = (value - high).astype(jnp.bfloat16).astype(jnp.float32)
    low = value - high - middle
    row = lax.broadcasted_iota(jnp.int32, (rows, EXTRA), 0)
    lines = jnp.where(row == 0, high, jnp.where(row == 1, middle, low))
    return jnp.where(row < 3, lines, 0.0).astype(jnp.bfloat16)


def joined_lines(lines):
    return jnp.sum(lines.astype(jnp.float32), axis=0, keepdims=True)


def total_kernel(replicas, outer_ref, moment_ref, own_ref, *refs):
    pseudo_ref, pack_ref = refs[-2:]
    outer = outer_ref[...]
    width = outer.shape[1]
    total = own_ref[...]
    for ref in refs[:-2]:
        total += ref[...].astype(jnp.float32)
    pseudo = outer - total / replicas
    pseudo_ref[...] = pseudo
    pack_ref[0, :, :width] = (outer - 0.567 * moment_ref[...]).astype(jnp.bfloat16)
    pack_ref[1, :, :width] = (1.33 * pseudo).astype(jnp.bfloat16)
    square_sum = jnp.sum(jnp.sum(pseudo * pseudo, axis=0, keepdims=True), keepdims=True)
    lines = split_lines(square_sum, outer.shape[0])
    pack_ref[0, :, width:] = lines
    pack_ref[1, :, width:] = lines


def join_kernel(*refs):
    pack_refs = refs[: len(JUMPS)]
    joined_ref, sums_hbm, sums_ref, sem = refs[len(JUMPS) :]
    width = joined_ref.shape[3]
    square_sum = sum(joined_lines(ref[0, :, width:]) for ref in pack_refs)
    sums_ref[...] = jnp.broadcast_to(square_sum[None], sums_ref.shape)
    copy = pltpu.make_async_copy(sums_ref, sums_hbm, sem)
    copy.start()
    for place, ref in enumerate(pack_refs):
        joined_ref[place] = ref[:, :, :width]
    copy.wait()


def source_kernel(max_norm, sums_ref, *refs):
    joined_refs, source_ref = refs[:-1], refs[-1]
    rows, width = joined_refs[0].shape[2:]
    square_sum = jnp.sum(sums_ref[:, 0, :1], axis=0, keepdims=True)
    factor = jnp.minimum(1.0, max_norm / (jnp.sqrt(square_sum) + 1e-06))
    lines = split_lines(factor, rows)
    for number, joined_ref in enumerate(joined_refs):
        for place in range(len(JUMPS)):
            base = joined_ref[place, 0].astype(jnp.float32)
            push = joined_ref[place, 1].astype(jnp.float32)
            source = base - factor * push
            source_ref[number, place, :, :width] = source.astype(jnp.bfloat16)
            source_ref[number, place, :, width:] = lines


def state_kernel(
    core,
    sources_ref,
    sources2_ref,
    outer_ref,
    moment_ref,
    pseudo_ref,
    pseudo2_ref,
    new_outer_ref,
    new_moment_ref,
):
    width = pseudo_ref.shape[1]
    for frag, lines_ref, rows_ref in (
        (core, sources_ref, pseudo_ref),
        (1 - core, sources2_ref, pseudo2_ref),
    ):
        factor = joined_lines(lines_ref[0, 0, :, width:])[:, :1]
        clipped = factor * rows_ref[...]
        moment = 0.9 * moment_ref[frag] + clipped
        new_moment_ref[frag] = moment
        new_outer_ref[frag] = outer_ref[frag] - 0.7 * (clipped + 0.9 * moment)


def mix_kernel(jobs, where_ref, weights_ref, *refs):
    core, zh, zl, yl = (where_ref[i] for i in range(4))
    mixed_hbm, mixed_ref, sems = refs
    stores = []
    for number, (source_ref, other_frag, other_z, other_y) in enumerate(jobs):
        frag = 1 - core if other_frag else core
        low = (1 - zl if other_z else zl) * 2 + (1 - yl if other_y else yl)
        for k, jump in enumerate(JUMPS):
            chip = 4 * (zh ^ jump) + low
            own = weights_ref[frag, chip].astype(jnp.float32)
            source = source_ref[k, :, : own.shape[1]].astype(jnp.float32)
            mixed_ref[number, k] = (0.5 * own + 0.5 * source).astype(jnp.bfloat16)
            stores.append(
                pltpu.make_async_copy(
                    mixed_ref.at[number, k], mixed_hbm.at[frag, chip], sems.at[number, k]
                )
            )
            stores[-1].start()
    for store in stores:
        store.wait()


def shards(local_weights, global_params, momentum):
    f32, bf16 = jnp.float32, jnp.bfloat16
    core = lax.axis_index("core")
    other = 1 - core
    first = core == 0
    chips = lax.axis_size(CHIPS)
    replicas = 2 * chips
    everywhere = lax.axis_size(EVERYWHERE)
    rows, width = local_weights.shape[3], local_weights.shape[4]
    share_rows = global_params.shape[2]
    block = rows // chips
    max_norm = 0.5 * math.sqrt(block * width * everywhere)

    def pick(array, index, axis=0):
        return lax.dynamic_index_in_dim(array, index, axis, keepdims=False)

    def swapped_rows(array):
        kept = pick(array, core)
        came = over_core(pick(array, other))
        return jnp.where(
            first,
            jnp.concatenate((kept, came), axis=0),
            jnp.concatenate((came, kept), axis=0),
        )

    weights = local_weights[:, 0, 0]
    outer = swapped_rows(global_params[:, 0])
    moment = swapped_rows(momentum[:, 0])
    sent = pl.pallas_call(
        cut_kernel,
        out_shape=pltpu.VMEM((rows, width), bf16),
        in_specs=[SMEM, ANY],
        out_specs=VMEM,
        scratch_shapes=[pltpu.SemaphoreType.DMA((PARTS,))],
        compiler_params=SMALL,
        name="cut",
    )(other[None], pltpu.with_memory_space_constraint(weights, pltpu.HBM))
    where = jnp.stack([core] + [lax.axis_index(axis) for axis in CHIPS])
    sizes = tuple(lax.axis_size(axis) for axis in CHIPS)
    half = width // 2
    spread = weights.reshape(2, *sizes, block, width)
    got = over_core(sent).reshape(*sizes, block, width)

    def reduced(kernel, outs, *given):
        return pl.pallas_call(
            kernel,
            out_shape=outs,
            in_specs=[SMEM] + [VMEM] * (2 + len(given)),
            out_specs=(VMEM,) * len(outs),
            compiler_params=SMALL,
            name="reduced",
        )(where, spread, got, *given)

    left, right = reduced(
        first_kernel, (pltpu.VMEM((sizes[0], 2, block, half), bf16),) * 2
    )
    left, right = over_y(left), over_z(right)
    left2, right2 = reduced(
        second_kernel, (pltpu.VMEM((sizes[0], block, half), bf16),) * 2, left, right
    )
    left2, right2 = over_z(left2), over_y(right2)
    own, *sums = reduced(
        third_kernel,
        (pltpu.VMEM((block, width), f32),)
        + (pltpu.VMEM((block, width), bf16),) * (len(JUMPS) - 1),
        left,
        right,
        left2,
        right2,
    )
    sums = [over("zh", 4, jump, one) for jump, one in zip(JUMPS[1:], sums)]
    pseudo, pack = pl.pallas_call(
        functools.partial(total_kernel, replicas),
        out_shape=(
            pltpu.VMEM((block, width), f32),
            pltpu.VMEM((2, block, width + EXTRA), bf16),
        ),
        in_specs=[VMEM] * (2 + len(JUMPS)),
        out_specs=(VMEM, VMEM),
        compiler_params=SMALL,
        name="total",
    )(outer, moment, own, *sums)
    halves = pseudo.reshape(2, share_rows, width)
    pseudo2 = over_core(pick(halves, other))

    packs = [pack] + [over("zh", 4, jump, pack) for jump in JUMPS[1:]]
    packs, pseudo2 = lax.optimization_barrier((packs, pseudo2))
    groups = lax.axis_size(GROUPS)
    joined, sums = pl.pallas_call(
        join_kernel,
        out_shape=(
            pltpu.VMEM((len(JUMPS), 2, block, width), bf16),
            jax.ShapeDtypeStruct((groups, 1, EXTRA), f32),
        ),
        in_specs=[VMEM] * len(JUMPS),
        out_specs=(VMEM, ANY),
        scratch_shapes=[
            pltpu.VMEM((groups, 1, EXTRA), f32),
            pltpu.SemaphoreType.DMA,
        ],
        compiler_params=SMALL,
        name="join",
    )(*packs)

    sums = lax.all_to_all(sums, GROUPS, 0, 0, tiled=True)
    after = over_z(joined)
    far = over_y(joined)
    sources = pl.pallas_call(
        functools.partial(source_kernel, max_norm),
        out_shape=pltpu.VMEM((3, len(JUMPS), block, width + EXTRA), bf16),
        in_specs=[VMEM] * 4,
        out_specs=VMEM,
        compiler_params=SMALL,
        name="source",
    )(sums, joined, after, far)

    left = over_y(sources[1, :, :, : width // 2])
    right = over_z(sources[2, :, :, width // 2 : width])
    sources2 = over_core(sources)

    blocks = weights.reshape(2, chips, block, width)

    def scratch(number):
        return [
            pltpu.VMEM((number, len(JUMPS), block, width), bf16),
            pltpu.SemaphoreType.DMA((number, len(JUMPS))),
        ]

    def mix_and_state(where_ref, weights_ref, sources_ref, sources2_ref, *refs):
        states, (mixed_hbm, *news), room = refs[:4], refs[4:7], refs[7:]
        jobs = [
            (ref.at[number], ref is sources2_ref, number == 1, number == 2)
            for number in range(3)
            for ref in (sources_ref, sources2_ref)
        ]
        mix_kernel(jobs, where_ref, weights_ref, mixed_hbm, *room)
        state_kernel(where_ref[0], sources_ref, sources2_ref, *states, *news)

    def mix_last(where_ref, weights_ref, source_ref, source2_ref, _, *refs):
        jobs = [(source_ref, False, True, True), (source2_ref, True, True, True)]
        mix_kernel(jobs, where_ref, weights_ref, *refs)

    state = jax.ShapeDtypeStruct((2, share_rows, width), f32)
    mixed_type = jax.ShapeDtypeStruct(blocks.shape, bf16)
    mixed, outer_next, moment_next = pl.pallas_call(
        mix_and_state,
        out_shape=(mixed_type, state, state),
        in_specs=[SMEM] + [VMEM] * 7,
        out_specs=(ANY, VMEM, VMEM),
        scratch_shapes=scratch(6),
        compiler_params=SMALL,
        name="mix",
    )(
        where,
        blocks,
        sources,
        sources2,
        global_params[:, 0],
        momentum[:, 0],
        pick(halves, core),
        pseudo2,
    )
    left, right, mixed = lax.optimization_barrier((left, right, mixed))
    diagonal = jnp.concatenate((left, right), axis=2)
    mixed = pl.pallas_call(
        mix_last,
        out_shape=mixed_type,
        in_specs=[SMEM, VMEM, VMEM, VMEM, ANY],
        out_specs=ANY,
        scratch_shapes=scratch(2),
        input_output_aliases={4: 0},
        compiler_params=SMALL,
        name="mix_last",
    )(where, blocks, diagonal, over_core(diagonal), mixed)
    return (
        mixed.reshape(local_weights.shape),
        outer_next[:, None],
        moment_next[:, None],
    )


def solution(mesh):
    fine = Mesh(
        mesh.devices.reshape(4, 2, 2, 2, 4, 2), ("zh", "zl", "yl", "core", "x", "yh")
    )
    replica, mp = ("zh", "zl", "yl", "core"), ("x", "yh")
    whole = P(None, replica, mp, None, None)
    outer = P(None, mp, replica, None)
    return jax.shard_map(
        shards,
        mesh=fine,
        in_specs=(whole, outer, outer),
        out_specs=(whole, outer, outer),
        check_vma=False,
    )
```

```python
import functools
import math

import jax
import jax.numpy as jnp
from jax import lax
from jax.experimental import pallas as pl
from jax.experimental.pallas import tpu as pltpu
from jax.sharding import Mesh
from jax.sharding import PartitionSpec as P

CHIPS = ("zh", "zl", "yl")
EVERYWHERE = ("zh", "zl", "yl", "x", "yh")
GROUPS = ("zl", "yl", "x", "yh")
JUMPS = (0, 2, 1, 3)
EXTRA = 128
PARTS = 4
ANY = pl.BlockSpec(memory_space=pl.ANY)
SMEM = pl.BlockSpec(memory_space=pltpu.SMEM)
SMALL = pltpu.CompilerParams(vmem_limit_bytes=12 * 1024 * 1024)
VMEM = pl.BlockSpec(memory_space=pltpu.VMEM)


def over(axis, size, jump, array):
    return lax.ppermute(array, axis, [(i, i ^ jump) for i in range(size)])


def over_core(array):
    return over("core", 2, 1, array)


def over_y(array):
    return over("yl", 2, 1, array)


def over_both(array):
    return over(("zl", "yl"), 4, 3, array)


def over_z(array):
    return over("zl", 2, 1, array)


def cut_kernel(which_ref, weights_hbm, cut_ref, sems):
    step = cut_ref.shape[0] // PARTS
    copies = []
    for part in range(PARTS):
        some = pl.ds(part * step, step)
        copies.append(
            pltpu.make_async_copy(
                weights_hbm.at[which_ref[0], some], cut_ref.at[some], sems.at[part]
            )
        )
        copies[-1].start()
    for copy in copies:
        copy.wait()


OTHERS = ((1, 0), (0, 1), (1, 1))


def pair_of(weights_ref, got_ref, core, at):
    own = weights_ref[(core, *at)].astype(jnp.float32)
    return own + got_ref[at].astype(jnp.float32)


def pairs_kernel(where_ref, weights_ref, got_ref, *outs):
    core, zl, yl = where_ref[0], where_ref[2], where_ref[3]
    for (to_z, to_y), out_ref in zip(OTHERS, outs):
        for zh in range(4):
            at = (zh, zl ^ to_z, yl ^ to_y)
            pair = pair_of(weights_ref, got_ref, core, at)
            out_ref[zh] = pair.astype(jnp.bfloat16)


def eights_kernel(where_ref, weights_ref, got_ref, *refs):
    core, zh, zl, yl = (where_ref[i] for i in range(4))
    came, outs = refs[: len(OTHERS)], refs[len(OTHERS) :]
    for jump, out_ref in zip(JUMPS, outs):
        to = zh ^ jump
        total = pair_of(weights_ref, got_ref, core, (to, zl, yl))
        for ref in came:
            total += ref[to].astype(jnp.float32)
        out_ref[...] = total.astype(out_ref.dtype)


def split_lines(value, rows):
    high = value.astype(jnp.bfloat16).astype(jnp.float32)
    middle = (value - high).astype(jnp.bfloat16).astype(jnp.float32)
    low = value - high - middle
    row = lax.broadcasted_iota(jnp.int32, (rows, EXTRA), 0)
    lines = jnp.where(row == 0, high, jnp.where(row == 1, middle, low))
    return jnp.where(row < 3, lines, 0.0).astype(jnp.bfloat16)


def joined_lines(lines):
    return jnp.sum(lines.astype(jnp.float32), axis=0, keepdims=True)


def total_kernel(replicas, outer_ref, moment_ref, own_ref, *refs):
    pseudo_ref, pack_ref = refs[-2:]
    outer = outer_ref[...]
    width = outer.shape[1]
    total = own_ref[...]
    for ref in refs[:-2]:
        total += ref[...].astype(jnp.float32)
    pseudo = outer - total / replicas
    pseudo_ref[...] = pseudo
    pack_ref[0, :, :width] = (outer - 0.567 * moment_ref[...]).astype(jnp.bfloat16)
    pack_ref[1, :, :width] = (1.33 * pseudo).astype(jnp.bfloat16)
    square_sum = jnp.sum(jnp.sum(pseudo * pseudo, axis=0, keepdims=True), keepdims=True)
    lines = split_lines(square_sum, outer.shape[0])
    pack_ref[0, :, width:] = lines
    pack_ref[1, :, width:] = lines


def join_kernel(*refs):
    pack_refs = refs[: len(JUMPS)]
    joined_ref, sums_hbm, sums_ref, sem = refs[len(JUMPS) :]
    width = joined_ref.shape[3]
    square_sum = sum(joined_lines(ref[0, :, width:]) for ref in pack_refs)
    sums_ref[...] = jnp.broadcast_to(square_sum[None], sums_ref.shape)
    copy = pltpu.make_async_copy(sums_ref, sums_hbm, sem)
    copy.start()
    for place, ref in enumerate(pack_refs):
        joined_ref[place] = ref[:, :, :width]
    copy.wait()


def source_kernel(max_norm, sums_ref, *refs):
    joined_refs, source_ref = refs[:-1], refs[-1]
    rows, width = joined_refs[0].shape[2:]
    square_sum = jnp.sum(sums_ref[:, 0, :1], axis=0, keepdims=True)
    factor = jnp.minimum(1.0, max_norm / (jnp.sqrt(square_sum) + 1e-06))
    lines = split_lines(factor, rows)
    for number, joined_ref in enumerate(joined_refs):
        for place in range(len(JUMPS)):
            base = joined_ref[place, 0].astype(jnp.float32)
            push = joined_ref[place, 1].astype(jnp.float32)
            source = base - factor * push
            source_ref[number, place, :, :width] = source.astype(jnp.bfloat16)
            source_ref[number, place, :, width:] = lines


def state_kernel(
    core,
    sources_ref,
    sources2_ref,
    outer_ref,
    moment_ref,
    pseudo_ref,
    pseudo2_ref,
    new_outer_ref,
    new_moment_ref,
):
    width = pseudo_ref.shape[1]
    for frag, lines_ref, rows_ref in (
        (core, sources_ref, pseudo_ref),
        (1 - core, sources2_ref, pseudo2_ref),
    ):
        factor = joined_lines(lines_ref[0, 0, :, width:])[:, :1]
        clipped = factor * rows_ref[...]
        moment = 0.9 * moment_ref[frag] + clipped
        new_moment_ref[frag] = moment
        new_outer_ref[frag] = outer_ref[frag] - 0.7 * (clipped + 0.9 * moment)


def mix_kernel(jobs, where_ref, weights_ref, *refs):
    core, zh, zl, yl = (where_ref[i] for i in range(4))
    mixed_hbm, mixed_ref, sems = refs
    stores = []
    for number, (source_ref, other_frag, other_z, other_y) in enumerate(jobs):
        frag = 1 - core if other_frag else core
        low = (1 - zl if other_z else zl) * 2 + (1 - yl if other_y else yl)
        for k, jump in enumerate(JUMPS):
            chip = 4 * (zh ^ jump) + low
            own = weights_ref[frag, chip].astype(jnp.float32)
            source = source_ref[k, :, : own.shape[1]].astype(jnp.float32)
            mixed_ref[number, k] = (0.5 * own + 0.5 * source).astype(jnp.bfloat16)
            stores.append(
                pltpu.make_async_copy(
                    mixed_ref.at[number, k], mixed_hbm.at[frag, chip], sems.at[number, k]
                )
            )
            stores[-1].start()
    for store in stores:
        store.wait()


def shards(local_weights, global_params, momentum):
    f32, bf16 = jnp.float32, jnp.bfloat16
    core = lax.axis_index("core")
    other = 1 - core
    first = core == 0
    chips = lax.axis_size(CHIPS)
    replicas = 2 * chips
    everywhere = lax.axis_size(EVERYWHERE)
    rows, width = local_weights.shape[3], local_weights.shape[4]
    share_rows = global_params.shape[2]
    block = rows // chips
    max_norm = 0.5 * math.sqrt(block * width * everywhere)

    def pick(array, index, axis=0):
        return lax.dynamic_index_in_dim(array, index, axis, keepdims=False)

    def swapped_rows(array):
        kept = pick(array, core)
        came = over_core(pick(array, other))
        return jnp.where(
            first,
            jnp.concatenate((kept, came), axis=0),
            jnp.concatenate((came, kept), axis=0),
        )

    weights = local_weights[:, 0, 0]
    outer = swapped_rows(global_params[:, 0])
    moment = swapped_rows(momentum[:, 0])
    sent = pl.pallas_call(
        cut_kernel,
        out_shape=pltpu.VMEM((rows, width), bf16),
        in_specs=[SMEM, ANY],
        out_specs=VMEM,
        scratch_shapes=[pltpu.SemaphoreType.DMA((PARTS,))],
        compiler_params=SMALL,
        name="cut",
    )(other[None], pltpu.with_memory_space_constraint(weights, pltpu.HBM))
    where = jnp.stack([core] + [lax.axis_index(axis) for axis in CHIPS])
    sizes = tuple(lax.axis_size(axis) for axis in CHIPS)
    half = width // 2
    spread = weights.reshape(2, *sizes, block, width)
    got = over_core(sent).reshape(*sizes, block, width)

    def reduced(kernel, outs, *given):
        return pl.pallas_call(
            kernel,
            out_shape=outs,
            in_specs=[SMEM] + [VMEM] * (2 + len(given)),
            out_specs=(VMEM,) * len(outs),
            compiler_params=SMALL,
            name="reduced",
        )(where, spread, got, *given)

    pairs = reduced(
        pairs_kernel, (pltpu.VMEM((sizes[0], block, width), bf16),) * len(OTHERS)
    )
    pairs = [over_z(pairs[0]), over_y(pairs[1]), over_both(pairs[2])]
    own, *sums = reduced(
        eights_kernel,
        (pltpu.VMEM((block, width), f32),)
        + (pltpu.VMEM((block, width), bf16),) * (len(JUMPS) - 1),
        *pairs,
    )
    sums = [over("zh", 4, jump, one) for jump, one in zip(JUMPS[1:], sums)]
    pseudo, pack = pl.pallas_call(
        functools.partial(total_kernel, replicas),
        out_shape=(
            pltpu.VMEM((block, width), f32),
            pltpu.VMEM((2, block, width + EXTRA), bf16),
        ),
        in_specs=[VMEM] * (2 + len(JUMPS)),
        out_specs=(VMEM, VMEM),
        compiler_params=SMALL,
        name="total",
    )(outer, moment, own, *sums)
    halves = pseudo.reshape(2, share_rows, width)
    pseudo2 = over_core(pick(halves, other))

    packs = [pack] + [over("zh", 4, jump, pack) for jump in JUMPS[1:]]
    packs, pseudo2 = lax.optimization_barrier((packs, pseudo2))
    groups = lax.axis_size(GROUPS)
    joined, sums = pl.pallas_call(
        join_kernel,
        out_shape=(
            pltpu.VMEM((len(JUMPS), 2, block, width), bf16),
            jax.ShapeDtypeStruct((groups, 1, EXTRA), f32),
        ),
        in_specs=[VMEM] * len(JUMPS),
        out_specs=(VMEM, ANY),
        scratch_shapes=[
            pltpu.VMEM((groups, 1, EXTRA), f32),
            pltpu.SemaphoreType.DMA,
        ],
        compiler_params=SMALL,
        name="join",
    )(*packs)

    sums = lax.all_to_all(sums, GROUPS, 0, 0, tiled=True)
    after = over_z(joined)
    far = over_y(joined)
    sources = pl.pallas_call(
        functools.partial(source_kernel, max_norm),
        out_shape=pltpu.VMEM((3, len(JUMPS), block, width + EXTRA), bf16),
        in_specs=[VMEM] * 4,
        out_specs=VMEM,
        compiler_params=SMALL,
        name="source",
    )(sums, joined, after, far)

    left = over_y(sources[1, :, :, : width // 2])
    right = over_z(sources[2, :, :, width // 2 : width])
    sources2 = over_core(sources)

    blocks = weights.reshape(2, chips, block, width)

    def scratch(number):
        return [
            pltpu.VMEM((number, len(JUMPS), block, width), bf16),
            pltpu.SemaphoreType.DMA((number, len(JUMPS))),
        ]

    def mix_and_state(where_ref, weights_ref, sources_ref, sources2_ref, *refs):
        states, (mixed_hbm, *news), room = refs[:4], refs[4:7], refs[7:]
        jobs = [
            (ref.at[number], ref is sources2_ref, number == 1, number == 2)
            for number in range(3)
            for ref in (sources_ref, sources2_ref)
        ]
        mix_kernel(jobs, where_ref, weights_ref, mixed_hbm, *room)
        state_kernel(where_ref[0], sources_ref, sources2_ref, *states, *news)

    def mix_last(where_ref, weights_ref, source_ref, source2_ref, _, *refs):
        jobs = [(source_ref, False, True, True), (source2_ref, True, True, True)]
        mix_kernel(jobs, where_ref, weights_ref, *refs)

    state = jax.ShapeDtypeStruct((2, share_rows, width), f32)
    mixed_type = jax.ShapeDtypeStruct(blocks.shape, bf16)
    mixed, outer_next, moment_next = pl.pallas_call(
        mix_and_state,
        out_shape=(mixed_type, state, state),
        in_specs=[SMEM] + [VMEM] * 7,
        out_specs=(ANY, VMEM, VMEM),
        scratch_shapes=scratch(6),
        compiler_params=SMALL,
        name="mix",
    )(
        where,
        blocks,
        sources,
        sources2,
        global_params[:, 0],
        momentum[:, 0],
        pick(halves, core),
        pseudo2,
    )
    left, right, mixed = lax.optimization_barrier((left, right, mixed))
    diagonal = jnp.concatenate((left, right), axis=2)
    mixed = pl.pallas_call(
        mix_last,
        out_shape=mixed_type,
        in_specs=[SMEM, VMEM, VMEM, VMEM, ANY],
        out_specs=ANY,
        scratch_shapes=scratch(2),
        input_output_aliases={4: 0},
        compiler_params=SMALL,
        name="mix_last",
    )(where, blocks, diagonal, over_core(diagonal), mixed)
    return (
        mixed.reshape(local_weights.shape),
        outer_next[:, None],
        moment_next[:, None],
    )


def solution(mesh):
    fine = Mesh(
        mesh.devices.reshape(4, 2, 2, 2, 4, 2), ("zh", "zl", "yl", "core", "x", "yh")
    )
    replica, mp = ("zh", "zl", "yl", "core"), ("x", "yh")
    whole = P(None, replica, mp, None, None)
    outer = P(None, mp, replica, None)
    return jax.shard_map(
        shards,
        mesh=fine,
        in_specs=(whole, outer, outer),
        out_specs=(whole, outer, outer),
        check_vma=False,
    )
```

```python
import functools
import math

import jax
import jax.numpy as jnp
from jax import lax
from jax.experimental import pallas as pl
from jax.experimental.pallas import tpu as pltpu
from jax.sharding import Mesh
from jax.sharding import PartitionSpec as P

CHIPS = ("zh", "zl", "yl")
EVERYWHERE = ("zh", "zl", "yl", "x", "yh")
GROUPS = ("zl", "yl", "x", "yh")
JUMPS = (0, 2, 1, 3)
EXTRA = 128
PARTS = 4
ANY = pl.BlockSpec(memory_space=pl.ANY)
SMEM = pl.BlockSpec(memory_space=pltpu.SMEM)
SMALL = pltpu.CompilerParams(vmem_limit_bytes=12 * 1024 * 1024)
VMEM = pl.BlockSpec(memory_space=pltpu.VMEM)


def over(axis, size, jump, array):
    return lax.ppermute(array, axis, [(i, i ^ jump) for i in range(size)])


def over_core(array):
    return over("core", 2, 1, array)


def over_y(array):
    return over("yl", 2, 1, array)


def over_both(array):
    return over(("zl", "yl"), 4, 3, array)


def over_z(array):
    return over("zl", 2, 1, array)


def cut_kernel(which_ref, weights_hbm, cut_ref, sems):
    step = cut_ref.shape[0] // PARTS
    copies = []
    for part in range(PARTS):
        some = pl.ds(part * step, step)
        copies.append(
            pltpu.make_async_copy(
                weights_hbm.at[which_ref[0], some], cut_ref.at[some], sems.at[part]
            )
        )
        copies[-1].start()
    for copy in copies:
        copy.wait()


OTHERS = ((1, 0), (0, 1), (1, 1))


def pair_of(weights_ref, got_ref, core, at):
    own = weights_ref[(core, *at)].astype(jnp.float32)
    return own + got_ref[at].astype(jnp.float32)


def pairs_kernel(where_ref, weights_ref, got_ref, *outs):
    core, zl, yl = where_ref[0], where_ref[2], where_ref[3]
    for (to_z, to_y), out_ref in zip(OTHERS, outs):
        for zh in range(4):
            at = (zh, zl ^ to_z, yl ^ to_y)
            out_ref[zh] = weights_ref[(core, *at)] + got_ref[at]


def eights_kernel(where_ref, weights_ref, got_ref, *refs):
    core, zh, zl, yl = (where_ref[i] for i in range(4))
    came, outs = refs[: len(OTHERS)], refs[len(OTHERS) :]
    for jump, out_ref in zip(JUMPS, outs):
        to = zh ^ jump
        total = pair_of(weights_ref, got_ref, core, (to, zl, yl))
        for ref in came:
            total += ref[to].astype(jnp.float32)
        out_ref[...] = total.astype(out_ref.dtype)


def split_lines(value, rows):
    high = value.astype(jnp.bfloat16).astype(jnp.float32)
    middle = (value - high).astype(jnp.bfloat16).astype(jnp.float32)
    low = value - high - middle
    row = lax.broadcasted_iota(jnp.int32, (rows, EXTRA), 0)
    lines = jnp.where(row == 0, high, jnp.where(row == 1, middle, low))
    return jnp.where(row < 3, lines, 0.0).astype(jnp.bfloat16)


def joined_lines(lines):
    return jnp.sum(lines.astype(jnp.float32), axis=0, keepdims=True)


def total_kernel(replicas, outer_ref, moment_ref, own_ref, *refs):
    pseudo_ref, pack_ref = refs[-2:]
    outer = outer_ref[...]
    width = outer.shape[1]
    total = own_ref[...]
    for ref in refs[:-2]:
        total += ref[...].astype(jnp.float32)
    pseudo = outer - total / replicas
    pseudo_ref[...] = pseudo
    pack_ref[0, :, :width] = (outer - 0.567 * moment_ref[...]).astype(jnp.bfloat16)
    pack_ref[1, :, :width] = (1.33 * pseudo).astype(jnp.bfloat16)
    square_sum = jnp.sum(jnp.sum(pseudo * pseudo, axis=0, keepdims=True), keepdims=True)
    lines = split_lines(square_sum, outer.shape[0])
    pack_ref[0, :, width:] = lines
    pack_ref[1, :, width:] = lines


def join_kernel(*refs):
    pack_refs = refs[: len(JUMPS)]
    joined_ref, sums_hbm, sums_ref, sem = refs[len(JUMPS) :]
    width = joined_ref.shape[3]
    square_sum = sum(joined_lines(ref[0, :, width:]) for ref in pack_refs)
    sums_ref[...] = jnp.broadcast_to(square_sum[None], sums_ref.shape)
    copy = pltpu.make_async_copy(sums_ref, sums_hbm, sem)
    copy.start()
    for place, ref in enumerate(pack_refs):
        joined_ref[place] = ref[:, :, :width]
    copy.wait()


def source_kernel(max_norm, sums_ref, *refs):
    joined_refs, source_ref = refs[:-1], refs[-1]
    rows, width = joined_refs[0].shape[2:]
    square_sum = jnp.sum(sums_ref[:, 0, :1], axis=0, keepdims=True)
    factor = jnp.minimum(1.0, max_norm / (jnp.sqrt(square_sum) + 1e-06))
    lines = split_lines(factor, rows)
    for number, joined_ref in enumerate(joined_refs):
        for place in range(len(JUMPS)):
            base = joined_ref[place, 0].astype(jnp.float32)
            push = joined_ref[place, 1].astype(jnp.float32)
            source = base - factor * push
            source_ref[number, place, :, :width] = source.astype(jnp.bfloat16)
            source_ref[number, place, :, width:] = lines


def state_kernel(
    core,
    sources_ref,
    sources2_ref,
    outer_ref,
    moment_ref,
    pseudo_ref,
    pseudo2_ref,
    new_outer_ref,
    new_moment_ref,
):
    width = pseudo_ref.shape[1]
    for frag, lines_ref, rows_ref in (
        (core, sources_ref, pseudo_ref),
        (1 - core, sources2_ref, pseudo2_ref),
    ):
        factor = joined_lines(lines_ref[0, 0, :, width:])[:, :1]
        clipped = factor * rows_ref[...]
        moment = 0.9 * moment_ref[frag] + clipped
        new_moment_ref[frag] = moment
        new_outer_ref[frag] = outer_ref[frag] - 0.7 * (clipped + 0.9 * moment)


def mix_kernel(jobs, where_ref, weights_ref, *refs):
    core, zh, zl, yl = (where_ref[i] for i in range(4))
    mixed_hbm, mixed_ref, sems = refs
    stores = []
    for number, (source_ref, other_frag, other_z, other_y) in enumerate(jobs):
        frag = 1 - core if other_frag else core
        low = (1 - zl if other_z else zl) * 2 + (1 - yl if other_y else yl)
        for k, jump in enumerate(JUMPS):
            chip = 4 * (zh ^ jump) + low
            own = weights_ref[frag, chip]
            source = source_ref[k, :, : own.shape[1]]
            mixed_ref[number, k] = jnp.bfloat16(0.5) * (own + source)
            stores.append(
                pltpu.make_async_copy(
                    mixed_ref.at[number, k], mixed_hbm.at[frag, chip], sems.at[number, k]
                )
            )
            stores[-1].start()
    for store in stores:
        store.wait()


def shards(local_weights, global_params, momentum):
    f32, bf16 = jnp.float32, jnp.bfloat16
    core = lax.axis_index("core")
    other = 1 - core
    first = core == 0
    chips = lax.axis_size(CHIPS)
    replicas = 2 * chips
    everywhere = lax.axis_size(EVERYWHERE)
    rows, width = local_weights.shape[3], local_weights.shape[4]
    share_rows = global_params.shape[2]
    block = rows // chips
    max_norm = 0.5 * math.sqrt(block * width * everywhere)

    def pick(array, index, axis=0):
        return lax.dynamic_index_in_dim(array, index, axis, keepdims=False)

    def swapped_rows(array):
        kept = pick(array, core)
        came = over_core(pick(array, other))
        return jnp.where(
            first,
            jnp.concatenate((kept, came), axis=0),
            jnp.concatenate((came, kept), axis=0),
        )

    weights = local_weights[:, 0, 0]
    outer = swapped_rows(global_params[:, 0])
    moment = swapped_rows(momentum[:, 0])
    sent = pl.pallas_call(
        cut_kernel,
        out_shape=pltpu.VMEM((rows, width), bf16),
        in_specs=[SMEM, ANY],
        out_specs=VMEM,
        scratch_shapes=[pltpu.SemaphoreType.DMA((PARTS,))],
        compiler_params=SMALL,
        name="cut",
    )(other[None], pltpu.with_memory_space_constraint(weights, pltpu.HBM))
    where = jnp.stack([core] + [lax.axis_index(axis) for axis in CHIPS])
    sizes = tuple(lax.axis_size(axis) for axis in CHIPS)
    half = width // 2
    spread = weights.reshape(2, *sizes, block, width)
    got = over_core(sent).reshape(*sizes, block, width)

    def reduced(kernel, outs, *given):
        return pl.pallas_call(
            kernel,
            out_shape=outs,
            in_specs=[SMEM] + [VMEM] * (2 + len(given)),
            out_specs=(VMEM,) * len(outs),
            compiler_params=SMALL,
            name="reduced",
        )(where, spread, got, *given)

    pairs = reduced(
        pairs_kernel, (pltpu.VMEM((sizes[0], block, width), bf16),) * len(OTHERS)
    )
    pairs = [over_z(pairs[0]), over_y(pairs[1]), over_both(pairs[2])]
    own, *sums = reduced(
        eights_kernel,
        (pltpu.VMEM((block, width), f32),)
        + (pltpu.VMEM((block, width), bf16),) * (len(JUMPS) - 1),
        *pairs,
    )
    sums = [over("zh", 4, jump, one) for jump, one in zip(JUMPS[1:], sums)]
    pseudo, pack = pl.pallas_call(
        functools.partial(total_kernel, replicas),
        out_shape=(
            pltpu.VMEM((block, width), f32),
            pltpu.VMEM((2, block, width + EXTRA), bf16),
        ),
        in_specs=[VMEM] * (2 + len(JUMPS)),
        out_specs=(VMEM, VMEM),
        compiler_params=SMALL,
        name="total",
    )(outer, moment, own, *sums)
    halves = pseudo.reshape(2, share_rows, width)
    pseudo2 = over_core(pick(halves, other))

    packs = [over("zh", 4, jump, pack) for jump in JUMPS[:0:-1]]
    packs, pseudo2 = lax.optimization_barrier((packs, pseudo2))
    packs = [pack] + packs[::-1]
    groups = lax.axis_size(GROUPS)
    joined, sums = pl.pallas_call(
        join_kernel,
        out_shape=(
            pltpu.VMEM((len(JUMPS), 2, block, width), bf16),
            jax.ShapeDtypeStruct((groups, 1, EXTRA), f32),
        ),
        in_specs=[VMEM] * len(JUMPS),
        out_specs=(VMEM, ANY),
        scratch_shapes=[
            pltpu.VMEM((groups, 1, EXTRA), f32),
            pltpu.SemaphoreType.DMA,
        ],
        compiler_params=SMALL,
        name="join",
    )(*packs)

    sums = lax.all_to_all(sums, GROUPS, 0, 0, tiled=True)
    after = over_z(joined)
    far = over_y(joined)
    sources = pl.pallas_call(
        functools.partial(source_kernel, max_norm),
        out_shape=pltpu.VMEM((3, len(JUMPS), block, width + EXTRA), bf16),
        in_specs=[VMEM] * 4,
        out_specs=VMEM,
        compiler_params=SMALL,
        name="source",
    )(sums, joined, after, far)

    left = over_y(sources[1, :, :, : width // 2])
    right = over_z(sources[2, :, :, width // 2 : width])
    sources2 = over_core(sources)

    blocks = weights.reshape(2, chips, block, width)

    def scratch(number):
        return [
            pltpu.VMEM((number, len(JUMPS), block, width), bf16),
            pltpu.SemaphoreType.DMA((number, len(JUMPS))),
        ]

    def mix_and_state(where_ref, weights_ref, sources_ref, sources2_ref, *refs):
        states, (mixed_hbm, *news), room = refs[:4], refs[4:7], refs[7:]
        jobs = [
            (ref.at[number], ref is sources2_ref, number == 1, number == 2)
            for number in range(3)
            for ref in (sources_ref, sources2_ref)
        ]
        mix_kernel(jobs, where_ref, weights_ref, mixed_hbm, *room)
        state_kernel(where_ref[0], sources_ref, sources2_ref, *states, *news)

    def mix_last(where_ref, weights_ref, source_ref, source2_ref, _, *refs):
        jobs = [(source_ref, False, True, True), (source2_ref, True, True, True)]
        mix_kernel(jobs, where_ref, weights_ref, *refs)

    state = jax.ShapeDtypeStruct((2, share_rows, width), f32)
    mixed_type = jax.ShapeDtypeStruct(blocks.shape, bf16)
    mixed, outer_next, moment_next = pl.pallas_call(
        mix_and_state,
        out_shape=(mixed_type, state, state),
        in_specs=[SMEM] + [VMEM] * 7,
        out_specs=(ANY, VMEM, VMEM),
        scratch_shapes=scratch(6),
        compiler_params=SMALL,
        name="mix",
    )(
        where,
        blocks,
        sources,
        sources2,
        global_params[:, 0],
        momentum[:, 0],
        pick(halves, core),
        pseudo2,
    )
    left, right, mixed = lax.optimization_barrier((left, right, mixed))
    diagonal = jnp.concatenate((left, right), axis=2)
    mixed = pl.pallas_call(
        mix_last,
        out_shape=mixed_type,
        in_specs=[SMEM, VMEM, VMEM, VMEM, ANY],
        out_specs=ANY,
        scratch_shapes=scratch(2),
        input_output_aliases={4: 0},
        compiler_params=SMALL,
        name="mix_last",
    )(where, blocks, diagonal, over_core(diagonal), mixed)
    return (
        mixed.reshape(local_weights.shape),
        outer_next[:, None],
        moment_next[:, None],
    )


def solution(mesh):
    fine = Mesh(
        mesh.devices.reshape(4, 2, 2, 2, 4, 2), ("zh", "zl", "yl", "core", "x", "yh")
    )
    replica, mp = ("zh", "zl", "yl", "core"), ("x", "yh")
    whole = P(None, replica, mp, None, None)
    outer = P(None, mp, replica, None)
    return jax.shard_map(
        shards,
        mesh=fine,
        in_specs=(whole, outer, outer),
        out_specs=(whole, outer, outer),
        check_vma=False,
    )
```

```python
import functools
import math

import jax
import jax.numpy as jnp
from jax import lax
from jax.experimental import pallas as pl
from jax.experimental.pallas import tpu as pltpu
from jax.sharding import Mesh
from jax.sharding import PartitionSpec as P

CHIPS = ("zh", "zl", "yl")
EVERYWHERE = ("zh", "zl", "yl", "x", "yh")
GROUPS = ("zl", "yl", "x", "yh")
JUMPS = (0, 2, 1, 3)
EXTRA = 128
PARTS = 4
ANY = pl.BlockSpec(memory_space=pl.ANY)
SMEM = pl.BlockSpec(memory_space=pltpu.SMEM)
SMALL = pltpu.CompilerParams(vmem_limit_bytes=12 * 1024 * 1024)
VMEM = pl.BlockSpec(memory_space=pltpu.VMEM)


def over(axis, size, jump, array):
    return lax.ppermute(array, axis, [(i, i ^ jump) for i in range(size)])


def over_core(array):
    return over("core", 2, 1, array)


def over_y(array):
    return over("yl", 2, 1, array)


def over_both(array):
    return over(("zl", "yl"), 4, 3, array)


def over_z(array):
    return over("zl", 2, 1, array)


def cut_kernel(which_ref, weights_hbm, cut_ref, sems):
    step = cut_ref.shape[0] // PARTS
    copies = []
    for part in range(PARTS):
        some = pl.ds(part * step, step)
        copies.append(
            pltpu.make_async_copy(
                weights_hbm.at[which_ref[0], some], cut_ref.at[some], sems.at[part]
            )
        )
        copies[-1].start()
    for copy in copies:
        copy.wait()


OTHERS = ((1, 0), (0, 1), (1, 1))


def pair_of(weights_ref, got_ref, core, at):
    own = weights_ref[(core, *at)].astype(jnp.float32)
    return own + got_ref[at].astype(jnp.float32)


def pairs_kernel(where_ref, weights_ref, got_ref, *outs):
    core, zl, yl = where_ref[0], where_ref[2], where_ref[3]
    for (to_z, to_y), out_ref in zip(OTHERS, outs):
        for zh in range(4):
            at = (zh, zl ^ to_z, yl ^ to_y)
            pair = pair_of(weights_ref, got_ref, core, at)
            out_ref[zh] = pair.astype(jnp.bfloat16)


def eights_kernel(where_ref, weights_ref, got_ref, *refs):
    core, zh, zl, yl = (where_ref[i] for i in range(4))
    came, outs = refs[: len(OTHERS)], refs[len(OTHERS) :]
    for jump, out_ref in zip(JUMPS, outs):
        to = zh ^ jump
        total = pair_of(weights_ref, got_ref, core, (to, zl, yl))
        for ref in came:
            total += ref[to].astype(jnp.float32)
        out_ref[...] = total.astype(out_ref.dtype)


def split_lines(value, rows):
    high = value.astype(jnp.bfloat16).astype(jnp.float32)
    middle = (value - high).astype(jnp.bfloat16).astype(jnp.float32)
    low = value - high - middle
    row = lax.broadcasted_iota(jnp.int32, (rows, EXTRA), 0)
    lines = jnp.where(row == 0, high, jnp.where(row == 1, middle, low))
    return jnp.where(row < 3, lines, 0.0).astype(jnp.bfloat16)


def joined_lines(lines):
    return jnp.sum(lines.astype(jnp.float32), axis=0, keepdims=True)


def total_kernel(replicas, outer_ref, moment_ref, own_ref, *refs):
    pseudo_ref, pack_ref = refs[-2:]
    outer = outer_ref[...]
    width = outer.shape[1]
    total = own_ref[...]
    for ref in refs[:-2]:
        total += ref[...].astype(jnp.float32)
    pseudo = outer - total / replicas
    pseudo_ref[...] = pseudo
    pack_ref[0, :, :width] = (outer - 0.567 * moment_ref[...]).astype(jnp.bfloat16)
    pack_ref[1, :, :width] = (1.33 * pseudo).astype(jnp.bfloat16)
    square_sum = jnp.sum(jnp.sum(pseudo * pseudo, axis=0, keepdims=True), keepdims=True)
    lines = split_lines(square_sum, outer.shape[0])
    pack_ref[0, :, width:] = lines
    pack_ref[1, :, width:] = lines


def join_kernel(*refs):
    pack_refs = refs[: len(JUMPS)]
    joined_ref, sums_hbm, sums_ref, sem = refs[len(JUMPS) :]
    width = joined_ref.shape[3]
    square_sum = sum(joined_lines(ref[0, :, width:]) for ref in pack_refs)
    sums_ref[...] = jnp.broadcast_to(square_sum[None], sums_ref.shape)
    copy = pltpu.make_async_copy(sums_ref, sums_hbm, sem)
    copy.start()
    for place, ref in enumerate(pack_refs):
        joined_ref[place] = ref[:, :, :width]
    copy.wait()


def source_kernel(max_norm, sums_ref, *refs):
    joined_refs, source_ref = (refs[0], refs[2], refs[1]), refs[-1]
    rows, width = joined_refs[0].shape[2:]
    square_sum = jnp.sum(sums_ref[:, 0, :1], axis=0, keepdims=True)
    factor = jnp.minimum(1.0, max_norm / (jnp.sqrt(square_sum) + 1e-06))
    lines = split_lines(factor, rows)
    for number, joined_ref in enumerate(joined_refs):
        for place in range(len(JUMPS)):
            base = joined_ref[place, 0].astype(jnp.float32)
            push = joined_ref[place, 1].astype(jnp.float32)
            source = base - factor * push
            source_ref[number, place, :, :width] = source.astype(jnp.bfloat16)
            source_ref[number, place, :, width:] = lines


def state_kernel(
    core,
    sources_ref,
    sources2_ref,
    outer_ref,
    moment_ref,
    pseudo_ref,
    pseudo2_ref,
    new_outer_ref,
    new_moment_ref,
):
    width = pseudo_ref.shape[1]
    for frag, lines_ref, rows_ref in (
        (core, sources_ref, pseudo_ref),
        (1 - core, sources2_ref, pseudo2_ref),
    ):
        factor = joined_lines(lines_ref[0, 0, :, width:])[:, :1]
        clipped = factor * rows_ref[...]
        moment = 0.9 * moment_ref[frag] + clipped
        new_moment_ref[frag] = moment
        new_outer_ref[frag] = outer_ref[frag] - 0.7 * (clipped + 0.9 * moment)


def mix_kernel(jobs, where_ref, weights_ref, *refs):
    core, zh, zl, yl = (where_ref[i] for i in range(4))
    mixed_hbm, mixed_ref, sems = refs
    stores = []
    for number, (source_ref, other_frag, other_z, other_y) in enumerate(jobs):
        frag = 1 - core if other_frag else core
        low = (1 - zl if other_z else zl) * 2 + (1 - yl if other_y else yl)
        for k, jump in enumerate(JUMPS):
            chip = 4 * (zh ^ jump) + low
            own = weights_ref[frag, chip].astype(jnp.float32)
            source = source_ref[k, :, : own.shape[1]].astype(jnp.float32)
            mixed_ref[number, k] = (0.5 * own + 0.5 * source).astype(jnp.bfloat16)
            stores.append(
                pltpu.make_async_copy(
                    mixed_ref.at[number, k], mixed_hbm.at[frag, chip], sems.at[number, k]
                )
            )
            stores[-1].start()
    for store in stores:
        store.wait()


def shards(local_weights, global_params, momentum):
    f32, bf16 = jnp.float32, jnp.bfloat16
    core = lax.axis_index("core")
    other = 1 - core
    first = core == 0
    chips = lax.axis_size(CHIPS)
    replicas = 2 * chips
    everywhere = lax.axis_size(EVERYWHERE)
    rows, width = local_weights.shape[3], local_weights.shape[4]
    share_rows = global_params.shape[2]
    block = rows // chips
    max_norm = 0.5 * math.sqrt(block * width * everywhere)

    def pick(array, index, axis=0):
        return lax.dynamic_index_in_dim(array, index, axis, keepdims=False)

    def swapped_rows(array):
        kept = pick(array, core)
        came = over_core(pick(array, other))
        return jnp.where(
            first,
            jnp.concatenate((kept, came), axis=0),
            jnp.concatenate((came, kept), axis=0),
        )

    weights = local_weights[:, 0, 0]
    outer = swapped_rows(global_params[:, 0])
    moment = swapped_rows(momentum[:, 0])
    sent = pl.pallas_call(
        cut_kernel,
        out_shape=pltpu.VMEM((rows, width), bf16),
        in_specs=[SMEM, ANY],
        out_specs=VMEM,
        scratch_shapes=[pltpu.SemaphoreType.DMA((PARTS,))],
        compiler_params=SMALL,
        name="cut",
    )(other[None], pltpu.with_memory_space_constraint(weights, pltpu.HBM))
    where = jnp.stack([core] + [lax.axis_index(axis) for axis in CHIPS])
    sizes = tuple(lax.axis_size(axis) for axis in CHIPS)
    half = width // 2
    spread = weights.reshape(2, *sizes, block, width)
    got = over_core(sent).reshape(*sizes, block, width)

    def reduced(kernel, outs, *given):
        return pl.pallas_call(
            kernel,
            out_shape=outs,
            in_specs=[SMEM] + [VMEM] * (2 + len(given)),
            out_specs=(VMEM,) * len(outs),
            compiler_params=SMALL,
            name="reduced",
        )(where, spread, got, *given)

    pairs = reduced(
        pairs_kernel, (pltpu.VMEM((sizes[0], block, width), bf16),) * len(OTHERS)
    )
    pairs = [over_z(pairs[0]), over_y(pairs[1]), over_both(pairs[2])]
    own, *sums = reduced(
        eights_kernel,
        (pltpu.VMEM((block, width), f32),)
        + (pltpu.VMEM((block, width), bf16),) * (len(JUMPS) - 1),
        *pairs,
    )
    sums = [over("zh", 4, jump, one) for jump, one in zip(JUMPS[1:], sums)]
    pseudo, pack = pl.pallas_call(
        functools.partial(total_kernel, replicas),
        out_shape=(
            pltpu.VMEM((block, width), f32),
            pltpu.VMEM((2, block, width + EXTRA), bf16),
        ),
        in_specs=[VMEM] * (2 + len(JUMPS)),
        out_specs=(VMEM, VMEM),
        compiler_params=SMALL,
        name="total",
    )(outer, moment, own, *sums)
    halves = pseudo.reshape(2, share_rows, width)
    pseudo2 = over_core(pick(halves, other))

    packs = [pack] + [over("zh", 4, jump, pack) for jump in JUMPS[1:]]
    packs, pseudo2 = lax.optimization_barrier((packs, pseudo2))
    groups = lax.axis_size(GROUPS)
    joined, sums = pl.pallas_call(
        join_kernel,
        out_shape=(
            pltpu.VMEM((len(JUMPS), 2, block, width), bf16),
            jax.ShapeDtypeStruct((groups, 1, EXTRA), f32),
        ),
        in_specs=[VMEM] * len(JUMPS),
        out_specs=(VMEM, ANY),
        scratch_shapes=[
            pltpu.VMEM((groups, 1, EXTRA), f32),
            pltpu.SemaphoreType.DMA,
        ],
        compiler_params=SMALL,
        name="join",
    )(*packs)

    sums = lax.all_to_all(sums, GROUPS, 0, 0, tiled=True)
    far = over_y(joined)
    after = over_z(joined)
    sources = pl.pallas_call(
        functools.partial(source_kernel, max_norm),
        out_shape=pltpu.VMEM((3, len(JUMPS), block, width + EXTRA), bf16),
        in_specs=[VMEM] * 4,
        out_specs=VMEM,
        compiler_params=SMALL,
        name="source",
    )(sums, joined, far, after)

    right = over_z(sources[2, :, :, width // 2 : width])
    left = over_y(sources[1, :, :, : width // 2])
    sources2 = over_core(sources)

    blocks = weights.reshape(2, chips, block, width)

    def scratch(number):
        return [
            pltpu.VMEM((number, len(JUMPS), block, width), bf16),
            pltpu.SemaphoreType.DMA((number, len(JUMPS))),
        ]

    def mix_and_state(where_ref, weights_ref, sources_ref, sources2_ref, *refs):
        states, (mixed_hbm, *news), room = refs[:4], refs[4:7], refs[7:]
        jobs = [
            (ref.at[number], ref is sources2_ref, number == 1, number == 2)
            for number in range(3)
            for ref in (sources_ref, sources2_ref)
        ]
        mix_kernel(jobs, where_ref, weights_ref, mixed_hbm, *room)
        state_kernel(where_ref[0], sources_ref, sources2_ref, *states, *news)

    def mix_last(where_ref, weights_ref, source_ref, source2_ref, _, *refs):
        jobs = [(source_ref, False, True, True), (source2_ref, True, True, True)]
        mix_kernel(jobs, where_ref, weights_ref, *refs)

    state = jax.ShapeDtypeStruct((2, share_rows, width), f32)
    mixed_type = jax.ShapeDtypeStruct(blocks.shape, bf16)
    mixed, outer_next, moment_next = pl.pallas_call(
        mix_and_state,
        out_shape=(mixed_type, state, state),
        in_specs=[SMEM] + [VMEM] * 7,
        out_specs=(ANY, VMEM, VMEM),
        scratch_shapes=scratch(6),
        compiler_params=SMALL,
        name="mix",
    )(
        where,
        blocks,
        sources,
        sources2,
        global_params[:, 0],
        momentum[:, 0],
        pick(halves, core),
        pseudo2,
    )
    left, right, mixed = lax.optimization_barrier((left, right, mixed))
    diagonal = jnp.concatenate((left, right), axis=2)
    mixed = pl.pallas_call(
        mix_last,
        out_shape=mixed_type,
        in_specs=[SMEM, VMEM, VMEM, VMEM, ANY],
        out_specs=ANY,
        scratch_shapes=scratch(2),
        input_output_aliases={4: 0},
        compiler_params=SMALL,
        name="mix_last",
    )(where, blocks, diagonal, over_core(diagonal), mixed)
    return (
        mixed.reshape(local_weights.shape),
        outer_next[:, None],
        moment_next[:, None],
    )


def solution(mesh):
    fine = Mesh(
        mesh.devices.reshape(4, 2, 2, 2, 4, 2), ("zh", "zl", "yl", "core", "x", "yh")
    )
    replica, mp = ("zh", "zl", "yl", "core"), ("x", "yh")
    whole = P(None, replica, mp, None, None)
    outer = P(None, mp, replica, None)
    return jax.shard_map(
        shards,
        mesh=fine,
        in_specs=(whole, outer, outer),
        out_specs=(whole, outer, outer),
        check_vma=False,
    )
```
